32 devices in a mesh: dp: 4 (over z), section: 2 (over y), mp: 4 (over x, core).
Axes of the slice: x: 2, y: 2, z: 4, core: 2. Of those that a mesh axis runs over, the one named last changes fastest.
Arguments:
- patches: bfloat16 [4, 2, 16, 16, 3200], P('dp', 'section'), may hold values from -6 to 6
- w_in: bfloat16 [3200, 3584], P(None, 'mp'), may hold values from -0.109375 to 0.109375
- ln_gain: float32 [3584], P('mp'), may hold values from 0.25 to 1.75
- ln_bias: float32 [3584], P('mp'), may hold values from -3 to 3
- dw_kernel: float32 [3, 3, 3584], P(None, None, 'mp'), may hold values from -2 to 2
- w_tube: bfloat16 [2, 2, 2, 3584, 3584], P('section', None, None, 'mp', 'dp'), may hold values from -0.03125 to 0.03125
- grad_out: bfloat16 [4, 64, 3584], P(None, None, 'dp'), may hold values from -6 to 6
- clip_frames: int32 [4], replicated, may hold values from 8 to 32, as said below
- clip_batch: int32 [4], replicated, may hold values from 0 to 3
Outputs:
- tubes: bfloat16 [4, 64, 3584], P(None, ('section', 'mp'), 'dp')
- grad_w_in: float32 [3200, 3584], P(None, ('mp', 'dp', 'section'))
- grad_gain: float32 [3584], P(('mp', 'dp', 'section'))
- grad_bias: float32 [3584], P(('mp', 'dp', 'section'))
- grad_dw: float32 [3, 3, 3584], P(None, None, ('mp', 'dp', 'section'))
- grad_w_tube: float32 [2, 2, 2, 3584, 3584], P('section', None, None, 'mp', 'dp')
The draws below stay inside these ranges and needn't reach their ends.
Inputs may be any that keep to these rules, and one draw needn't show every extreme that they name: `clip_frames`: even numbers; their halves sum to 4 or more.
All inputs are finite; a program needn't handle non-finite values.
Results may differ from the reference program's by a relative error of at most 0.005.
Values may be sent and summed in bfloat16 or wider, within the bound.
No kernel may reach another device: no remote copies, remote signals or barrier semaphores. Data moves between devices by JAX's collectives and lax.ppermute only.
A program may use at most 128 MiB of HBM per device.

```python
import jax
import jax.numpy as jnp
from jax import lax

D_IN = 3200
CH = 3584
GRID = 16
MICRO = 4
NPAIR = 4
NCLIP = 4


def draw_clip_frames(key, part):
    first, second = jax.random.split(key)
    halves = jax.random.randint(first, (NCLIP,), 4, 17)
    order = jax.random.permutation(second, NCLIP)
    halves = halves.at[order[0]].set(16)
    if NCLIP > 1:
        halves = halves.at[order[1]].set(4)
    return (2 * halves).astype(jnp.int32)


def plant(entries, own_key, least, top_value):
    index_at = [jax.random.randint(jax.random.fold_in(own_key, axis), (), 0, length) for axis, length in enumerate(entries.shape)]
    widest = entries.shape.index(max(entries.shape))
    next_to = index_at[:widest] + [(index_at[widest] + 1) % entries.shape[widest]] + index_at[widest + 1:]
    return entries.at[tuple(index_at)].set(least).at[tuple(next_to)].set(top_value)


def block_levels(own_key, dims, pieces, least, top_value):
    loudness, own = 1.0, jax.random.fold_in(own_key, 6)
    for axis_at, shards_of in pieces:
        draws = jnp.exp(jax.random.uniform(jax.random.fold_in(own, axis_at), (shards_of,), jnp.float32, least / len(pieces), top_value / len(pieces)))
        loudness = loudness * jnp.repeat(draws, dims[axis_at] // shards_of).reshape([-1 if axis == axis_at else 1 for axis in range(len(dims))])
    return loudness


def gaussian(key, dims, spread, most, cuts=(), kind=jnp.bfloat16):
    loudness = block_levels(key, dims, cuts, -0.22, 0.18) if cuts else 1.0
    entries = jax.random.normal(key, dims, jnp.float32) * spread * loudness
    return jnp.minimum(jnp.maximum(entries, -most), most).astype(kind)


def setup_inputs(seed: int = 0) -> dict:
    seeds = jax.random.split(jax.random.key(seed), 10)
    patches = gaussian(seeds[0], (NPAIR, 2, GRID, GRID, D_IN), 1.0, 6.0, ((0, 4), (1, 2)))
    w_in = gaussian(seeds[1], (D_IN, CH), D_IN ** -0.5, 0.109375, ((1, 4),))
    ln_gain = jnp.clip(1.0 + 0.15 * jax.random.normal(seeds[2], (CH,), jnp.float32), 0.25, 1.75)
    ln_bias = gaussian(seeds[3], (CH,), 0.5, 3.0, ((0, 4),), jnp.float32)
    dw_kernel = gaussian(seeds[4], (3, 3, CH), 9 ** -0.5, 2.0, ((2, 4),), jnp.float32)
    w_tube = gaussian(seeds[5], (2, 2, 2, CH, CH), (8 * CH) ** -0.5, 0.03125, ((0, 2), (3, 4), (4, 4)))
    grad_out = gaussian(seeds[6], (NPAIR, (GRID // 2) * (GRID // 2), CH), 1.0, 6.0, ((2, 4),))
    clip_frames = draw_clip_frames(jax.random.fold_in(seeds[9], 71), 0)
    clip_batch = plant(jax.random.randint(seeds[8], (NCLIP,), 0, MICRO), jax.random.fold_in(seeds[8], 1), 0, MICRO - 1).astype(jnp.int32)
    return {"patches": patches, "w_in": w_in, "ln_gain": ln_gain, "ln_bias": ln_bias, "dw_kernel": dw_kernel, "w_tube": w_tube, "grad_out": grad_out, "clip_frames": clip_frames, "clip_batch": clip_batch}


EPS = 1e-06

def silu_slope(value):
    sig = jax.nn.sigmoid(value)
    return sig * (1.0 + value * (1.0 - sig))

def pair_scale(clip_frames, clip_batch, count, nclip):
    halves = (clip_frames // 2).astype(jnp.int32)
    ends = jnp.cumsum(halves).astype(jnp.int32)
    starts = (ends - halves).astype(jnp.int32)
    places = jnp.arange(count, dtype=jnp.int32)
    member = ((places[:, None] >= starts[None, :]) & (places[:, None] < ends[None, :])).astype(jnp.float32)
    batch_hot = (clip_batch[:, None] == jnp.arange(MICRO, dtype=jnp.int32)[None, :]).astype(jnp.float32)
    batch_pairs = lax.optimization_barrier(jnp.sum(batch_hot * halves.astype(jnp.float32)[:, None], axis=0))
    clip_load = lax.optimization_barrier(jnp.sum(batch_hot * batch_pairs[None, :], axis=1))
    clip_scale = 10.0 * nclip / (MICRO * clip_load)
    return lax.optimization_barrier(jnp.sum(member * clip_scale[None, :], axis=1))

def reference(patches, w_in, ln_gain, ln_bias, dw_kernel, w_tube, grad_out, clip_frames, clip_batch):
    half = GRID // 2
    rows = patches.reshape(NPAIR * 2 * GRID * GRID, D_IN)
    pre = jnp.dot(rows, w_in, preferred_element_type=jnp.float32)
    mean = lax.optimization_barrier(jnp.mean(pre, axis=1, keepdims=True))
    centered = pre - mean
    var = lax.optimization_barrier(jnp.mean(centered * centered, axis=1, keepdims=True))
    rstd = lax.rsqrt(var + EPS)
    normed = centered * rstd
    shifted = normed * ln_gain + ln_bias
    act = jax.nn.silu(shifted).reshape(NPAIR * 2, GRID, GRID, CH)
    padded = jnp.pad(act, ((0, 0), (1, 1), (1, 1), (0, 0)))
    mixed = jnp.zeros_like(act)
    for upos in range(3):
        for vpos in range(3):
            mixed = mixed + dw_kernel[upos, vpos] * padded[:, upos:upos + GRID, vpos:vpos + GRID]
    maps = (act + jax.nn.silu(mixed)).astype(jnp.bfloat16)
    blocks = maps.reshape(NPAIR, 2, half, 2, half, 2, CH).transpose(0, 2, 4, 1, 3, 5, 6).reshape(NPAIR * half * half, 8 * CH)
    kernel = w_tube.reshape(8 * CH, CH)
    tubes = jnp.dot(blocks, kernel, preferred_element_type=jnp.float32).astype(jnp.bfloat16).reshape(NPAIR, half * half, CH)
    weight = pair_scale(clip_frames, clip_batch, NPAIR, NCLIP)
    upstream = (grad_out.astype(jnp.float32) * weight[:, None, None]).astype(jnp.bfloat16).reshape(NPAIR * half * half, CH)
    grad_w_tube = lax.dot_general(blocks, upstream, (((0,), (0,)), ((), ())), preferred_element_type=jnp.float32).reshape(2, 2, 2, CH, CH)
    grad_blocks = lax.dot_general(upstream, kernel, (((1,), (1,)), ((), ())), preferred_element_type=jnp.float32)
    grad_maps = grad_blocks.reshape(NPAIR, half, half, 2, 2, 2, CH).transpose(0, 3, 1, 4, 2, 5, 6).reshape(NPAIR * 2, GRID, GRID, CH)
    grad_mixed = grad_maps * silu_slope(mixed)
    grad_pad = jnp.pad(grad_mixed, ((0, 0), (1, 1), (1, 1), (0, 0)))
    grad_act = grad_maps
    kernel_rows = []
    for upos in range(3):
        for vpos in range(3):
            grad_act = grad_act + dw_kernel[upos, vpos] * grad_pad[:, 2 - upos:2 - upos + GRID, 2 - vpos:2 - vpos + GRID]
            kernel_rows.append(lax.optimization_barrier(jnp.sum(grad_mixed * padded[:, upos:upos + GRID, vpos:vpos + GRID], axis=(0, 1, 2))))
    grad_dw = jnp.stack(kernel_rows).reshape(3, 3, CH)
    grad_shift = grad_act.reshape(-1, CH) * silu_slope(shifted)
    grad_gain = lax.optimization_barrier(jnp.sum(grad_shift * normed, axis=0))
    grad_bias = lax.optimization_barrier(jnp.sum(grad_shift, axis=0))
    scaled = grad_shift * ln_gain
    grad_pre = (scaled - lax.optimization_barrier(jnp.mean(scaled, axis=1, keepdims=True)) - normed * lax.optimization_barrier(jnp.mean(scaled * normed, axis=1, keepdims=True))) * rstd
    grad_w_in = lax.dot_general(rows, grad_pre.astype(jnp.bfloat16), (((0,), (0,)), ((), ())), preferred_element_type=jnp.float32)
    return (tubes, grad_w_in, grad_gain, grad_bias, grad_dw, grad_w_tube)
```

```python
import functools

import jax
import jax.numpy as jnp
from jax import lax
from jax.experimental import pallas as pl
from jax.experimental.pallas import tpu as pltpu
from jax.sharding import PartitionSpec as P

CH = 3584
MICRO = 4
EPS = 1e-06
LANES = 128
BF = jnp.bfloat16
F32 = jnp.float32
CORE = [(0, 1), (1, 0), (2, 3), (3, 2)]
CROSS = [(0, 2), (2, 0), (1, 3), (3, 1)]
TAP = {(u, a): ((u + a) % 2, (u + a) // 2) for u in range(2) for a in (-1, 0, 1)}


def params(mib):
    return pltpu.CompilerParams(vmem_limit_bytes=mib * 2**20)


def pair_scale(clip_frames, clip_batch, count, nclip):
    halves = clip_frames // 2
    ends = jnp.cumsum(halves)
    starts = ends - halves
    places = jnp.arange(count, dtype=jnp.int32)
    member = ((places[:, None] >= starts[None, :]) & (places[:, None] < ends[None, :])).astype(F32)
    batch_hot = (clip_batch[:, None] == jnp.arange(MICRO, dtype=jnp.int32)[None, :]).astype(F32)
    batch_pairs = jnp.sum(batch_hot * halves.astype(F32)[:, None], axis=0)
    clip_load = jnp.sum(batch_hot * batch_pairs[None, :], axis=1)
    clip_scale = 10.0 * nclip / (MICRO * clip_load)
    return jnp.sum(member * clip_scale[None, :], axis=1)


def sigmoid(value):
    return 0.5 + 0.5 * jnp.tanh(0.5 * value)


def columns_to_rows(columns):
    rows = columns[0].shape[0]
    lane = lax.broadcasted_iota(jnp.int32, (rows, LANES), 1)
    wide = jnp.zeros((rows, LANES), F32)
    for place, column in enumerate(columns):
        wide = jnp.where(lane == place, column, wide)
    return wide.T[:8]


def rows_to_columns(stacked):
    padded = jnp.concatenate([stacked, jnp.zeros((LANES - 8, stacked.shape[1]), F32)], axis=0)
    turned = padded.T
    return [turned[:, place : place + 1] for place in range(8)]


def term_kernel(up_ref, w_ref, out_ref):
    pairs, _, cells, width = out_ref.shape
    value = lax.dot_general(
        up_ref[...], w_ref[0], (((1,), (1,)), ((), ())), preferred_element_type=F32
    )
    out_ref[...] = value.astype(BF).reshape(pairs, 1, cells, width)


def term_call(upstream, kernel, cells):
    rows, out_width = upstream.shape
    phases, width, _ = kernel.shape
    pairs = rows // cells
    return pl.pallas_call(
        term_kernel,
        grid=(phases,),
        in_specs=[
            pl.BlockSpec((rows, out_width), lambda q: (0, 0)),
            pl.BlockSpec((1, width, out_width), lambda q: (q, 0, 0)),
        ],
        out_specs=pl.BlockSpec((pairs, 1, cells, width), lambda q: (0, q, 0, 0)),
        out_shape=jax.ShapeDtypeStruct((pairs, phases, cells, width), BF),
        compiler_params=params(32),
        cost_estimate=pl.CostEstimate(
            flops=2 * rows * phases * width * out_width,
            bytes_accessed=2 * phases * width * (out_width + rows),
            transcendentals=0,
        ),
        name="term",
    )(upstream, kernel)


def pre_kernel(groups, order_ref, *refs):
    pieces, (w_ref, pre_ref, stat_ref, total_ref) = refs[: 4 * groups], refs[4 * groups :]
    step, steps = pl.program_id(0), pl.num_programs(0)
    cells = pieces[0].shape[0]
    width = w_ref.shape[1]
    frame = 4 * cells
    for group in range(groups):
        rows = jnp.concatenate([ref[...] for ref in pieces[4 * group : 4 * group + 4]], axis=0)
        value = jnp.dot(rows, w_ref[...], preferred_element_type=F32)

        @pl.when(step == 0)
        def _():
            total_ref[group] = value

        @pl.when(step > 0)
        def _():
            total_ref[group] += value

    @pl.when(step == steps - 1)
    def _():
        for group in range(groups):
            for place in range(4):
                pre_ref[group, order_ref[place]] = total_ref[
                    group, place * cells : (place + 1) * cells
                ]
            value = pre_ref[group].reshape(frame, width)
            mean = jnp.sum(value, axis=1, keepdims=True) * (1.0 / width)
            apart = value - mean
            spread = jnp.sum(apart * apart, axis=1, keepdims=True)
            stat_ref[group] = columns_to_rows([mean, spread])


def pre_call(order, groups, w_in, chunk):
    depth, width = w_in.shape
    cells = groups[0][0].shape[0]
    count = len(groups)
    pieces = [piece for group in groups for piece in group]
    return pl.pallas_call(
        functools.partial(pre_kernel, count),
        grid_spec=pltpu.PrefetchScalarGridSpec(
            num_scalar_prefetch=1,
            grid=(depth // chunk,),
            in_specs=[pl.BlockSpec((cells, chunk), lambda k, order: (0, k)) for _ in pieces]
            + [pl.BlockSpec((chunk, width), lambda k, order: (k, 0))],
            out_specs=[
                pl.BlockSpec((count, 4, cells, width), lambda k, order: (0, 0, 0, 0)),
                pl.BlockSpec((count, 8, 4 * cells), lambda k, order: (0, 0, 0)),
            ],
            scratch_shapes=[pltpu.VMEM((count, 4 * cells, width), F32)],
        ),
        out_shape=[
            jax.ShapeDtypeStruct((count, 4, cells, width), F32),
            jax.ShapeDtypeStruct((count, 8, 4 * cells), F32),
        ],
        compiler_params=params(52),
        cost_estimate=pl.CostEstimate(
            flops=8 * count * cells * depth * width,
            bytes_accessed=2 * depth * (width + 4 * count * cells),
            transcendentals=0,
        ),
        name="pre",
    )(order, *pieces, w_in)


def spread_stats(stats, width, mean_ref, rstd_ref):
    blocks = stats.shape[0]
    means, spreads = stats[:, 0], stats[:, 1]
    mean = jnp.sum(means, axis=0, keepdims=True) * (1.0 / blocks)
    apart = means - mean
    total = jnp.sum(spreads, axis=0, keepdims=True) + width * jnp.sum(
        apart * apart, axis=0, keepdims=True
    )
    rstd = lax.rsqrt(total * (1.0 / (width * blocks)) + EPS)
    row = lax.broadcasted_iota(jnp.int32, (8, mean.shape[1]), 0)
    column = rows_to_columns(jnp.where(row == 0, mean, jnp.where(row == 1, rstd, 0.0)))
    mean_ref[...] = jnp.broadcast_to(column[0], mean_ref.shape)
    rstd_ref[...] = jnp.broadcast_to(column[1], rstd_ref.shape)


def shift_rows(value, by):
    if by == 0:
        return value
    empty = jnp.zeros_like(value[:1])
    if by < 0:
        return jnp.concatenate([empty, value[:-1]], axis=0)
    return jnp.concatenate([value[1:], empty], axis=0)


def shift_columns(value, by):
    if by == 0:
        return value
    half = value.shape[1]
    place = lax.broadcasted_iota(jnp.int32, value.shape, 1)
    if by < 0:
        return jnp.where(place == 0, 0.0, pltpu.roll(value, 1, 1))
    return jnp.where(place == half - 1, 0.0, pltpu.roll(value, half - 1, 1))


def neighbours(grid_values):
    sides = {}
    for u in range(2):
        for v in range(2):
            for by in (0, -1 if v == 1 else 1):
                sides[u, v, by] = shift_columns(grid_values[u, v], by)
    found = {}
    for u in range(2):
        for v in range(2):
            for a in (-1, 0, 1):
                for b in (-1, 0, 1):
                    row, by_row = TAP[u, a]
                    column, by_column = TAP[v, b]
                    found[u, v, a, b] = shift_rows(sides[row, column, by_column], by_row)
    return found


def forward(pre, mean, rstd, gain, bias, taps, half):
    cells = half * half
    normed, shifted, sig, act, mixed = {}, {}, {}, {}, {}
    for u in range(2):
        for v in range(2):
            place = 2 * u + v
            rows = slice(place * cells, (place + 1) * cells)
            value = (pre[place] - mean[rows]) * rstd[rows]
            moved = value * gain + bias
            gate = sigmoid(moved)
            normed[u, v], shifted[u, v], sig[u, v] = value, moved, gate
            act[u, v] = (moved * gate).reshape(half, half, LANES)
    around = neighbours(act)
    for u in range(2):
        for v in range(2):
            total = None
            for a in (-1, 0, 1):
                for b in (-1, 0, 1):
                    part = taps[a + 1][b + 1] * around[u, v, a, b]
                    total = part if total is None else total + part
            mixed[u, v] = total
    return normed, shifted, sig, act, mixed, around


def load_taps(dw_ref):
    return [[dw_ref[3 * a + b : 3 * a + b + 1] for b in range(3)] for a in range(3)]


def maps_kernel(half, total_width, pre_ref, stat_ref, gain_ref, bias_ref, dw_ref, maps_ref, mean_ref, rstd_ref):
    cells = half * half

    @pl.when(pl.program_id(1) == 0)
    def _():
        spread_stats(stat_ref[0], total_width, mean_ref, rstd_ref)

    _, _, _, act, mixed, _ = forward(
        pre_ref[0], mean_ref[...], rstd_ref[...], gain_ref[...], bias_ref[...], load_taps(dw_ref), half
    )
    for u in range(2):
        for v in range(2):
            value = mixed[u, v]
            maps = act[u, v] + value * sigmoid(value)
            maps_ref[0, 2 * u + v] = maps.reshape(cells, LANES).astype(BF)


def maps_call(pre, stats, gain, bias, dw, half):
    count, phases, cells, width = pre.shape
    blocks = stats.shape[1]
    row = pl.BlockSpec((1, LANES), lambda p, c: (0, c))
    block = pl.BlockSpec((1, phases, cells, LANES), lambda p, c: (p, 0, 0, c))
    return pl.pallas_call(
        functools.partial(maps_kernel, half, width),
        grid=(count, width // LANES),
        in_specs=[
            block,
            pl.BlockSpec((1, blocks, 8, phases * cells), lambda p, c: (p, 0, 0, 0)),
            row,
            row,
            pl.BlockSpec((9, LANES), lambda p, c: (0, c)),
        ],
        out_specs=block,
        out_shape=jax.ShapeDtypeStruct(pre.shape, BF),
        scratch_shapes=[pltpu.VMEM((phases * cells, LANES), F32)] * 2,
        compiler_params=params(24),
        cost_estimate=pl.CostEstimate(
            flops=60 * pre.size, bytes_accessed=6 * pre.size, transcendentals=2 * pre.size
        ),
        name="maps",
    )(pre, stats, gain, bias, dw)


def tube_kernel(own_ref, others_ref, up_ref, w_ref, grad_ref, part_ref, total_ref):
    step, steps = pl.program_id(0), pl.num_programs(0)
    cells, width = own_ref.shape[2:]
    pairs = 1 + others_ref.shape[0]
    rows = jnp.concatenate(
        [own_ref[0, 0]] + [others_ref[place, 0] for place in range(pairs - 1)], axis=0
    )
    value = jnp.dot(rows, w_ref[0], preferred_element_type=F32)

    @pl.when(step == 0)
    def _():
        total_ref[...] = value

    @pl.when(step > 0)
    def _():
        total_ref[...] += value

    grad_ref[0] = lax.dot_general(
        rows, up_ref[...], (((0,), (0,)), ((), ())), preferred_element_type=F32
    )

    @pl.when(step == steps - 1)
    def _():
        owners, held = part_ref.shape[0], cells // part_ref.shape[0]
        for owner in range(owners):
            part_ref[owner] = jnp.concatenate(
                [
                    total_ref[pair * cells + owner * held : pair * cells + (owner + 1) * held]
                    for pair in range(pairs)
                ],
                axis=0,
            ).astype(BF)


def tube_call(own, others, upstream, kernel, owners):
    phases, cells, width = own.shape[1:]
    rows, out_width = upstream.shape
    return pl.pallas_call(
        tube_kernel,
        grid=(phases,),
        in_specs=[
            pl.BlockSpec((1, 1, cells, width), lambda q: (0, q, 0, 0)),
            pl.BlockSpec((others.shape[0], 1, cells, width), lambda q: (0, q, 0, 0)),
            pl.BlockSpec((rows, out_width), lambda q: (0, 0)),
            pl.BlockSpec((1, width, out_width), lambda q: (q, 0, 0)),
        ],
        out_specs=[
            pl.BlockSpec((1, width, out_width), lambda q: (q, 0, 0)),
            pl.BlockSpec((owners, rows // owners, out_width), lambda q: (0, 0, 0)),
        ],
        out_shape=[
            jax.ShapeDtypeStruct((phases, width, out_width), F32),
            jax.ShapeDtypeStruct((owners, rows // owners, out_width), BF),
        ],
        scratch_shapes=[pltpu.VMEM((rows, out_width), F32)],
        compiler_params=params(40),
        cost_estimate=pl.CostEstimate(
            flops=4 * rows * phases * width * out_width,
            bytes_accessed=6 * phases * width * out_width,
            transcendentals=0,
        ),
        name="tube",
    )(own, others, upstream, kernel)


def back_kernel(
    half, total_width, pre_ref, stat_ref, grad_ref, gain_ref, bias_ref, dw_ref,
    scaled_ref, sums_ref, back_ref, mean_ref, rstd_ref, first_ref, second_ref,
):
    step, steps = pl.program_id(0), pl.num_programs(0)
    cells = half * half

    @pl.when(step == 0)
    def _():
        spread_stats(stat_ref[0], total_width, mean_ref, rstd_ref)
        first_ref[...] = jnp.zeros_like(first_ref)
        second_ref[...] = jnp.zeros_like(second_ref)

    taps = load_taps(dw_ref)
    gain = gain_ref[...]
    normed, shifted, sig, _, mixed, around = forward(
        pre_ref[0], mean_ref[...], rstd_ref[...], gain, bias_ref[...], taps, half
    )
    grad_maps, grad_mixed = {}, {}
    for u in range(2):
        for v in range(2):
            value = mixed[u, v]
            gate = sigmoid(value)
            slope = gate * (1.0 + value * (1.0 - gate))
            grad = grad_ref[0, 2 * u + v].astype(F32).reshape(half, half, LANES)
            grad_maps[u, v] = grad
            grad_mixed[u, v] = grad * slope
    for a in (-1, 0, 1):
        for b in (-1, 0, 1):
            total = None
            for u in range(2):
                for v in range(2):
                    part = grad_mixed[u, v] * around[u, v, a, b]
                    total = part if total is None else total + part
            place = 3 * (a + 1) + b + 1
            sums_ref[place : place + 1] = jnp.sum(
                total.reshape(cells, LANES), axis=0, keepdims=True
            )
    spread = neighbours(grad_mixed)
    gain_total, bias_total = None, None
    for u in range(2):
        for v in range(2):
            total = grad_maps[u, v]
            for a in (-1, 0, 1):
                for b in (-1, 0, 1):
                    total = total + taps[a + 1][b + 1] * spread[u, v, -a, -b]
            gate, value = sig[u, v], shifted[u, v]
            grad_shift = total.reshape(cells, LANES) * (gate * (1.0 + value * (1.0 - gate)))
            along = grad_shift * normed[u, v]
            gain_total = along if gain_total is None else gain_total + along
            bias_total = grad_shift if bias_total is None else bias_total + grad_shift
            scaled = grad_shift * gain
            rows = slice((2 * u + v) * cells, (2 * u + v + 1) * cells)
            scaled_ref[rows] = scaled
            first_ref[rows] += scaled
            second_ref[rows] += along * gain
    sums_ref[9:10] = jnp.sum(gain_total, axis=0, keepdims=True)
    sums_ref[10:11] = jnp.sum(bias_total, axis=0, keepdims=True)
    sums_ref[11:16] = jnp.zeros((5, LANES), F32)

    @pl.when(step == steps - 1)
    def _():
        back_ref[...] = columns_to_rows(
            [
                jnp.sum(first_ref[...], axis=1, keepdims=True),
                jnp.sum(second_ref[...], axis=1, keepdims=True),
            ]
        )


def back_call(pre, stats, grad_maps, gain, bias, dw, half):
    _, phases, cells, width = pre.shape
    blocks = stats.shape[1]
    tokens = phases * cells
    row = pl.BlockSpec((1, LANES), lambda c: (0, c))
    block = pl.BlockSpec((1, phases, cells, LANES), lambda c: (0, 0, 0, c))
    return pl.pallas_call(
        functools.partial(back_kernel, half, width),
        grid=(width // LANES,),
        in_specs=[
            block,
            pl.BlockSpec((1, blocks, 8, tokens), lambda c: (0, 0, 0, 0)),
            block,
            row,
            row,
            pl.BlockSpec((9, LANES), lambda c: (0, c)),
        ],
        out_specs=[
            pl.BlockSpec((tokens, LANES), lambda c: (0, c)),
            pl.BlockSpec((16, LANES), lambda c: (0, c)),
            pl.BlockSpec((8, tokens), lambda c: (0, 0)),
        ],
        out_shape=[
            jax.ShapeDtypeStruct((tokens, width), F32),
            jax.ShapeDtypeStruct((16, width), F32),
            jax.ShapeDtypeStruct((8, tokens), F32),
        ],
        scratch_shapes=[pltpu.VMEM((tokens, LANES), F32)] * 4,
        compiler_params=params(24),
        cost_estimate=pl.CostEstimate(
            flops=150 * pre.size, bytes_accessed=10 * pre.size, transcendentals=2 * pre.size
        ),
        name="back",
    )(pre, stats, grad_maps, gain, bias, dw)


def turn_kernel(
    total_width, scaled_ref, pre_ref, stat_ref, back_ref, sums_ref, out_ref, mean_ref, rstd_ref, first_ref, second_ref
):
    tokens, width = scaled_ref.shape
    owners, rows, _ = out_ref.shape
    share = width // owners
    spread_stats(stat_ref[0], total_width, mean_ref, rstd_ref)
    column = rows_to_columns(
        jnp.sum(back_ref[...], axis=0) * (1.0 / (total_width * back_ref.shape[0]))
    )
    first_ref[...] = jnp.broadcast_to(column[0], first_ref.shape)
    second_ref[...] = jnp.broadcast_to(column[1], second_ref.shape)
    mean, rstd, first, second = mean_ref[...], rstd_ref[...], first_ref[...], second_ref[...]
    for part in range(width // LANES):
        lanes = slice(part * LANES, (part + 1) * LANES)
        normed = (pre_ref[0, :, :, lanes].reshape(tokens, LANES) - mean) * rstd
        grad = ((scaled_ref[:, lanes] - first - normed * second) * rstd).T.astype(BF)
        row = part * LANES
        while row < (part + 1) * LANES:
            owner, place = divmod(row, share)
            count = min(share - place, (part + 1) * LANES - row)
            out_ref[owner, place : place + count] = grad[row - part * LANES : row - part * LANES + count]
            row += count
    for owner in range(owners):
        value = sums_ref[:, owner * share : (owner + 1) * share]
        large = value.astype(BF)
        small = (value - large.astype(F32)).astype(BF)
        edge = jnp.zeros((16, LANES - share), BF)
        out_ref[owner, rows - 16 :, :LANES] = jnp.concatenate([large, edge], axis=1)
        out_ref[owner, rows - 16 :, LANES:] = jnp.concatenate([small, edge], axis=1)


def turn_call(scaled, pre, stats, back, sums, owners):
    tokens, width = scaled.shape
    rows = -(-(width // owners) // 16) * 16 + 16
    return pl.pallas_call(
        functools.partial(turn_kernel, width),
        out_shape=jax.ShapeDtypeStruct((owners, rows, tokens), BF),
        scratch_shapes=[pltpu.VMEM((tokens, LANES), F32)] * 4,
        compiler_params=params(24),
        cost_estimate=pl.CostEstimate(
            flops=8 * scaled.size, bytes_accessed=10 * scaled.size, transcendentals=0
        ),
        name="turn",
    )(scaled, pre, stats, back, sums)


def weight_kernel(groups, info_ref, *refs):
    pieces, (grad_ref, out_ref, sums_ref, rows_ref) = refs[: 4 * groups], refs[4 * groups :]
    cells = pieces[0].shape[0]
    frame = 4 * cells
    share = out_ref.shape[1]

    @pl.when(pl.program_id(0) == 0)
    def _():
        own = info_ref[0]
        for group in range(groups):
            value = grad_ref[info_ref[1 + group], :share].astype(F32)
            if group:
                value = jnp.where((own & 2) == 2, pltpu.roll(value, 2 * cells, 1), value)
                part = lax.broadcasted_iota(jnp.int32, value.shape, 1) // cells
                swapped = jnp.where(
                    (part & 1) == 0, pltpu.roll(value, 3 * cells, 1), pltpu.roll(value, cells, 1)
                )
                value = jnp.where((own & 1) == 1, swapped, value)
            rows_ref[:share, group * frame : (group + 1) * frame] = value.astype(BF)
        if share < LANES:
            rows_ref[share:] = jnp.zeros((LANES - share, groups * frame), BF)
        total = jnp.zeros((16, LANES), F32)
        for group in range(groups):
            tail = grad_ref[group, grad_ref.shape[1] - 16 :].astype(F32)
            total = total + tail[:, :LANES] + tail[:, LANES : 2 * LANES]
        sums_ref[...] = total

    patches = jnp.concatenate([ref[...] for ref in pieces], axis=0)
    value = jnp.dot(rows_ref[...], patches, preferred_element_type=F32)
    out_ref[...] = value.T[:, :share]


def weight_call(info, groups, grad, share, chunk):
    count, rows, tokens = grad.shape
    cells, depth = groups[0][0].shape
    pieces = [piece for group in groups for piece in group]
    return pl.pallas_call(
        functools.partial(weight_kernel, count),
        grid_spec=pltpu.PrefetchScalarGridSpec(
            num_scalar_prefetch=1,
            grid=(depth // chunk,),
            in_specs=[pl.BlockSpec((cells, chunk), lambda k, info: (0, k)) for _ in pieces]
            + [pl.BlockSpec((count, rows, tokens), lambda k, info: (0, 0, 0))],
            out_specs=[
                pl.BlockSpec((chunk, share), lambda k, info: (k, 0)),
                pl.BlockSpec((16, LANES), lambda k, info: (0, 0)),
            ],
            scratch_shapes=[pltpu.VMEM((LANES, count * tokens), BF)],
        ),
        out_shape=[
            jax.ShapeDtypeStruct((depth, share), F32),
            jax.ShapeDtypeStruct((16, LANES), F32),
        ],
        compiler_params=params(48),
        cost_estimate=pl.CostEstimate(
            flops=2 * LANES * count * tokens * depth,
            bytes_accessed=2 * count * tokens * depth,
            transcendentals=0,
        ),
        name="weight",
    )(info, *pieces, grad)


def shards(patches, w_in, ln_gain, ln_bias, dw_kernel, w_tube, grad_out, clip_frames, clip_batch):
    ranks, sections, blocks = lax.axis_size("dp"), lax.axis_size("section"), lax.axis_size("mp")
    rank, side, own = lax.axis_index("dp"), lax.axis_index("section"), lax.axis_index("mp")
    grid, depth = patches.shape[2], patches.shape[4]
    half = grid // 2
    cells = half * half
    width = w_in.shape[1]
    out_width = w_tube.shape[4]
    total_pairs = grad_out.shape[0]
    chunk = depth // 5
    share = width // (ranks * sections)
    gain, bias = ln_gain[None, :], ln_bias[None, :]
    dw = dw_kernel.reshape(9, width)
    kernel = w_tube.reshape(4, width, out_width)
    order = own ^ jnp.arange(4, dtype=jnp.int32)
    swap = [(i, (i + 1) % sections) for i in range(sections)]

    split = patches.reshape(half, 2, half, 2, depth)

    def phase(place):
        return lax.dynamic_slice(
            split, (0, place // 2, 0, place % 2, 0), (half, 1, half, 1, depth)
        ).reshape(cells, depth)

    piece = phase(own)
    piece, grad_out, patches = lax.optimization_barrier((piece, grad_out, patches))
    hops = sorted(range(1, ranks), key=lambda k: (min(k, ranks - k), k))
    fetched = [lax.ppermute(piece, "dp", [(i, (i + k) % ranks) for i in range(ranks)]) for k in hops]

    def shared(value):
        other = lax.ppermute(value, "mp", CROSS)
        return [value, lax.ppermute(value, "mp", CORE), other, lax.ppermute(other, "mp", CORE)]

    own_phases = [split[:, u, :, v].reshape(cells, depth) for u in range(2) for v in range(2)]
    groups = [shared(value) for value in fetched]
    across = [shared(lax.ppermute(value, "section", swap)) for value in [piece] + fetched]
    source = jnp.stack([rank] + [(rank - k) % ranks for k in hops])

    weight = pair_scale(clip_frames, clip_batch, total_pairs, clip_frames.shape[0])
    upstream = (grad_out.astype(F32) * weight[:, None, None]).astype(BF)
    term = term_call(upstream.reshape(total_pairs * cells, out_width), kernel, cells)
    term = lax.optimization_barrier((term, fetched))[0]
    grad_maps = lax.psum_scatter(term, "dp", scatter_dimension=0, tiled=True)

    def norm_stats(stat):
        return lax.all_gather(stat, "mp", axis=1)

    own_pre, own_stat = pre_call(jnp.arange(4, dtype=jnp.int32), [own_phases], w_in, chunk)
    own_stat = norm_stats(own_stat)
    own_maps = maps_call(own_pre, own_stat, gain, bias, dw, half)
    pre, stat = pre_call(order, groups, w_in, chunk)
    maps = maps_call(pre, norm_stats(stat), gain, bias, dw, half)

    near = jnp.take(upstream, source, axis=0).reshape(total_pairs * cells, out_width)
    grad_w_tube, partial = tube_call(own_maps, maps, near, kernel, sections * blocks)
    partial = lax.all_to_all(partial, ("section", "mp"), 0, 0, tiled=True)
    rows = jnp.sum(partial.astype(F32), axis=0).astype(BF).reshape(total_pairs, -1, out_width)
    tubes = jnp.zeros_like(rows).at[source].set(rows)

    scaled, sums, back = back_call(own_pre, own_stat, grad_maps, gain, bias, dw, half)
    back = lax.all_gather(back, "mp", axis=0)
    turned = turn_call(scaled, own_pre, own_stat, back, sums, ranks * sections)
    received = lax.all_to_all(turned, ("dp", "section"), 0, 0, tiled=True)
    place = jnp.concatenate([source * sections + side, source * sections + (sections - 1 - side)])
    info = jnp.concatenate([own[None], place]).astype(jnp.int32)
    grad_w_in, owned = weight_call(info, [own_phases] + groups + across, received, share, chunk)
    owned = owned[:, :share]
    return (
        tubes,
        grad_w_in,
        owned[9],
        owned[10],
        owned[:9].reshape(3, 3, -1),
        grad_w_tube.reshape(w_tube.shape),
    )


def solution(mesh):
    placed = (
        P("dp", "section", None, None, None),
        P(None, "mp"),
        P("mp"),
        P("mp"),
        P(None, None, "mp"),
        P("section", None, None, "mp", "dp"),
        P(None, None, "dp"),
        P(),
        P(),
    )
    return jax.shard_map(
        shards,
        mesh=mesh,
        in_specs=placed,
        out_specs=(
            P(None, ("section", "mp"), "dp"),
            P(None, ("mp", "dp", "section")),
            P(("mp", "dp", "section")),
            P(("mp", "dp", "section")),
            P(None, None, ("mp", "dp", "section")),
            P("section", None, None, "mp", "dp"),
        ),
        check_vma=False,
    )
```

```python
import functools

import jax
import jax.numpy as jnp
from jax import lax
from jax.experimental import pallas as pl
from jax.experimental.pallas import tpu as pltpu
from jax.sharding import PartitionSpec as P

CH = 3584
MICRO = 4
EPS = 1e-06
LANES = 128
BF = jnp.bfloat16
F32 = jnp.float32
CORE = [(0, 1), (1, 0), (2, 3), (3, 2)]
CROSS = [(0, 2), (2, 0), (1, 3), (3, 1)]
TAP = {(u, a): ((u + a) % 2, (u + a) // 2) for u in range(2) for a in (-1, 0, 1)}


def params(mib):
    return pltpu.CompilerParams(vmem_limit_bytes=mib * 2**20)


def pair_scale(clip_frames, clip_batch, count, nclip):
    halves = clip_frames // 2
    ends = jnp.cumsum(halves)
    starts = ends - halves
    places = jnp.arange(count, dtype=jnp.int32)
    member = ((places[:, None] >= starts[None, :]) & (places[:, None] < ends[None, :])).astype(F32)
    batch_hot = (clip_batch[:, None] == jnp.arange(MICRO, dtype=jnp.int32)[None, :]).astype(F32)
    batch_pairs = jnp.sum(batch_hot * halves.astype(F32)[:, None], axis=0)
    clip_load = jnp.sum(batch_hot * batch_pairs[None, :], axis=1)
    clip_scale = 10.0 * nclip / (MICRO * clip_load)
    return jnp.sum(member * clip_scale[None, :], axis=1)


def sigmoid(value):
    return 0.5 + 0.5 * jnp.tanh(0.5 * value)


def columns_to_rows(columns):
    rows = columns[0].shape[0]
    lane = lax.broadcasted_iota(jnp.int32, (rows, LANES), 1)
    wide = jnp.zeros((rows, LANES), F32)
    for place, column in enumerate(columns):
        wide = jnp.where(lane == place, column, wide)
    return wide.T[:8]


def rows_to_columns(stacked):
    padded = jnp.concatenate([stacked, jnp.zeros((LANES - 8, stacked.shape[1]), F32)], axis=0)
    turned = padded.T
    return [turned[:, place : place + 1] for place in range(8)]


def term_kernel(up_ref, w_ref, out_ref):
    pairs, _, cells, width = out_ref.shape
    value = lax.dot_general(
        up_ref[...], w_ref[0], (((1,), (1,)), ((), ())), preferred_element_type=F32
    )
    out_ref[...] = value.astype(BF).reshape(pairs, 1, cells, width)


def term_call(upstream, kernel, cells):
    rows, out_width = upstream.shape
    phases, width, _ = kernel.shape
    pairs = rows // cells
    return pl.pallas_call(
        term_kernel,
        grid=(phases,),
        in_specs=[
            pl.BlockSpec((rows, out_width), lambda q: (0, 0)),
            pl.BlockSpec((1, width, out_width), lambda q: (q, 0, 0)),
        ],
        out_specs=pl.BlockSpec((pairs, 1, cells, width), lambda q: (0, q, 0, 0)),
        out_shape=jax.ShapeDtypeStruct((pairs, phases, cells, width), BF),
        compiler_params=params(60),
        cost_estimate=pl.CostEstimate(
            flops=2 * rows * phases * width * out_width,
            bytes_accessed=2 * phases * width * (out_width + rows),
            transcendentals=0,
        ),
        name="term",
    )(upstream, kernel)


def phase_rows(shape, first, half):
    row = lax.broadcasted_iota(jnp.int32, shape, 0) + first * half * half
    token = lax.broadcasted_iota(jnp.int32, shape, 1)
    phase, cell = row // (half * half), row % (half * half)
    wanted = 2 * half * (2 * (cell // half) + phase // 2) + 2 * (cell % half) + phase % 2
    return jnp.where(token == wanted, 1.0, 0.0).astype(BF)


def phase_kernel(half, first_ref, rows_ref, out_ref):
    hot = phase_rows((out_ref.shape[0], rows_ref.shape[0]), first_ref[0], half)
    out_ref[...] = jnp.dot(hot, rows_ref[...], preferred_element_type=F32).astype(BF)


def phase_call(first, rows, count, half):
    tokens, depth = rows.shape
    out_rows = count * half * half
    return pl.pallas_call(
        functools.partial(phase_kernel, half),
        grid_spec=pltpu.PrefetchScalarGridSpec(
            num_scalar_prefetch=1,
            grid=(1,),
            in_specs=[pl.BlockSpec((tokens, depth), lambda k, first: (0, 0))],
            out_specs=pl.BlockSpec((out_rows, depth), lambda k, first: (0, 0)),
        ),
        out_shape=jax.ShapeDtypeStruct((out_rows, depth), BF),
        compiler_params=params(12),
        cost_estimate=pl.CostEstimate(
            flops=2 * tokens * out_rows * depth,
            bytes_accessed=2 * depth * (tokens + out_rows),
            transcendentals=0,
        ),
        name="phase",
    )(first, rows)


def pre_kernel(groups, each, order_ref, *refs):
    pieces, (w_ref, pre_ref, stat_ref) = refs[: each * groups], refs[each * groups :]
    width = w_ref.shape[1]
    cells = pre_ref.shape[2]
    frame = 4 * cells
    rows = jnp.concatenate([ref[...] for ref in pieces], axis=0)
    value = jnp.dot(rows, w_ref[...], preferred_element_type=F32)
    for group in range(groups):
        for place in range(4):
            start = group * frame + place * cells
            pre_ref[group, order_ref[place]] = value[start : start + cells]
        part = pre_ref[group].reshape(frame, width)
        mean = jnp.sum(part, axis=1, keepdims=True) * (1.0 / width)
        apart = part - mean
        spread = jnp.sum(apart * apart, axis=1, keepdims=True)
        stat_ref[group] = columns_to_rows([mean, spread])


def pre_call(order, groups, w_in, cells):
    depth, width = w_in.shape
    count, each = len(groups), len(groups[0])
    pieces = [piece for group in groups for piece in group]
    return pl.pallas_call(
        functools.partial(pre_kernel, count, each),
        grid_spec=pltpu.PrefetchScalarGridSpec(
            num_scalar_prefetch=1,
            grid=(),
            in_specs=[pl.BlockSpec(memory_space=pltpu.VMEM)] * (len(pieces) + 1),
            out_specs=[pl.BlockSpec(memory_space=pltpu.VMEM)] * 2,
        ),
        out_shape=[
            jax.ShapeDtypeStruct((count, 4, cells, width), F32),
            jax.ShapeDtypeStruct((count, 8, 4 * cells), F32),
        ],
        compiler_params=params(12),
        cost_estimate=pl.CostEstimate(
            flops=8 * count * cells * depth * width,
            bytes_accessed=2 * depth * (width + 4 * count * cells),
            transcendentals=0,
        ),
        name="pre",
    )(order, *pieces, w_in)


def spread_stats(stats, width, mean_ref, rstd_ref):
    blocks = stats.shape[0]
    means, spreads = stats[:, 0], stats[:, 1]
    mean = jnp.sum(means, axis=0, keepdims=True) * (1.0 / blocks)
    apart = means - mean
    total = jnp.sum(spreads, axis=0, keepdims=True) + width * jnp.sum(
        apart * apart, axis=0, keepdims=True
    )
    rstd = lax.rsqrt(total * (1.0 / (width * blocks)) + EPS)
    row = lax.broadcasted_iota(jnp.int32, (8, mean.shape[1]), 0)
    column = rows_to_columns(jnp.where(row == 0, mean, jnp.where(row == 1, rstd, 0.0)))
    mean_ref[...] = jnp.broadcast_to(column[0], mean_ref.shape)
    rstd_ref[...] = jnp.broadcast_to(column[1], rstd_ref.shape)


def shift_rows(value, by):
    if by == 0:
        return value
    empty = jnp.zeros_like(value[:1])
    if by < 0:
        return jnp.concatenate([empty, value[:-1]], axis=0)
    return jnp.concatenate([value[1:], empty], axis=0)


def shift_columns(value, by):
    if by == 0:
        return value
    half = value.shape[1]
    place = lax.broadcasted_iota(jnp.int32, value.shape, 1)
    if by < 0:
        return jnp.where(place == 0, 0.0, pltpu.roll(value, 1, 1))
    return jnp.where(place == half - 1, 0.0, pltpu.roll(value, half - 1, 1))


def neighbours(grid_values):
    sides = {}
    for u in range(2):
        for v in range(2):
            for by in (0, -1 if v == 1 else 1):
                sides[u, v, by] = shift_columns(grid_values[u, v], by)
    found = {}
    for u in range(2):
        for v in range(2):
            for a in (-1, 0, 1):
                for b in (-1, 0, 1):
                    row, by_row = TAP[u, a]
                    column, by_column = TAP[v, b]
                    found[u, v, a, b] = shift_rows(sides[row, column, by_column], by_row)
    return found


def forward(pre, mean, rstd, gain, bias, taps, half):
    cells = half * half
    normed, shifted, sig, act, mixed = {}, {}, {}, {}, {}
    for u in range(2):
        for v in range(2):
            place = 2 * u + v
            rows = slice(place * cells, (place + 1) * cells)
            value = (pre[place] - mean[rows]) * rstd[rows]
            moved = value * gain + bias
            gate = sigmoid(moved)
            normed[u, v], shifted[u, v], sig[u, v] = value, moved, gate
            act[u, v] = (moved * gate).reshape(half, half, LANES)
    around = neighbours(act)
    for u in range(2):
        for v in range(2):
            total = None
            for a in (-1, 0, 1):
                for b in (-1, 0, 1):
                    part = taps[a + 1][b + 1] * around[u, v, a, b]
                    total = part if total is None else total + part
            mixed[u, v] = total
    return normed, shifted, sig, act, mixed, around


def load_taps(dw_ref):
    return [[dw_ref[3 * a + b : 3 * a + b + 1] for b in range(3)] for a in range(3)]


def maps_kernel(half, total_width, pre_ref, stat_ref, gain_ref, bias_ref, dw_ref, maps_ref, mean_ref, rstd_ref):
    cells = half * half

    @pl.when(pl.program_id(1) == 0)
    def _():
        spread_stats(stat_ref[0], total_width, mean_ref, rstd_ref)

    _, _, _, act, mixed, _ = forward(
        pre_ref[0], mean_ref[...], rstd_ref[...], gain_ref[...], bias_ref[...], load_taps(dw_ref), half
    )
    for u in range(2):
        for v in range(2):
            value = mixed[u, v]
            maps = act[u, v] + value * sigmoid(value)
            maps_ref[0, 2 * u + v] = maps.reshape(cells, LANES).astype(BF)


def maps_call(pre, stats, gain, bias, dw, half):
    count, phases, cells, width = pre.shape
    blocks = stats.shape[1]
    row = pl.BlockSpec((1, LANES), lambda p, c: (0, c))
    block = pl.BlockSpec((1, phases, cells, LANES), lambda p, c: (p, 0, 0, c))
    return pl.pallas_call(
        functools.partial(maps_kernel, half, width),
        grid=(count, width // LANES),
        in_specs=[
            block,
            pl.BlockSpec((1, blocks, 8, phases * cells), lambda p, c: (p, 0, 0, 0)),
            row,
            row,
            pl.BlockSpec((9, LANES), lambda p, c: (0, c)),
        ],
        out_specs=block,
        out_shape=jax.ShapeDtypeStruct(pre.shape, BF),
        scratch_shapes=[pltpu.VMEM((phases * cells, LANES), F32)] * 2,
        compiler_params=params(8),
        cost_estimate=pl.CostEstimate(
            flops=60 * pre.size, bytes_accessed=6 * pre.size, transcendentals=2 * pre.size
        ),
        name="maps",
    )(pre, stats, gain, bias, dw)


def tube_kernel(count, source_ref, *refs):
    maps_refs = refs[:count]
    up_ref, w_ref, grad_ref, part_ref, total_ref, near_ref, sorted_ref = refs[count:]
    step, steps = pl.program_id(0), pl.num_programs(0)
    cells = maps_refs[0].shape[2]
    pairs = up_ref.shape[0]
    rows = jnp.concatenate([ref[i, 0] for ref in maps_refs for i in range(ref.shape[0])], axis=0)

    @pl.when(step == 0)
    def _():
        for pair in range(pairs):
            near_ref[pair * cells : (pair + 1) * cells] = up_ref[source_ref[pair]]

    value = jnp.dot(rows, w_ref[0], preferred_element_type=F32)

    @pl.when(step == 0)
    def _():
        total_ref[...] = value

    @pl.when(step > 0)
    def _():
        total_ref[...] += value

    grad_ref[0] = lax.dot_general(
        rows, near_ref[...], (((0,), (0,)), ((), ())), preferred_element_type=F32
    )

    @pl.when(step == steps - 1)
    def _():
        owners, held = part_ref.shape[0], cells // part_ref.shape[0]
        for pair in range(pairs):
            sorted_ref[source_ref[pair]] = total_ref[pair * cells : (pair + 1) * cells]
        for owner in range(owners):
            part_ref[owner] = jnp.concatenate(
                [sorted_ref[pair, owner * held : (owner + 1) * held] for pair in range(pairs)], axis=0
            ).astype(BF)


def tube_call(source, maps, upstream, kernel, owners):
    phases, cells, width = maps[0].shape[1:]
    pairs, _, out_width = upstream.shape
    rows = pairs * cells
    return pl.pallas_call(
        functools.partial(tube_kernel, len(maps)),
        grid_spec=pltpu.PrefetchScalarGridSpec(
            num_scalar_prefetch=1,
            grid=(phases,),
            in_specs=[
                pl.BlockSpec((value.shape[0], 1, cells, width), lambda q, source: (0, q, 0, 0))
                for value in maps
            ]
            + [
                pl.BlockSpec((pairs, cells, out_width), lambda q, source: (0, 0, 0)),
                pl.BlockSpec((1, width, out_width), lambda q, source: (q, 0, 0)),
            ],
            out_specs=[
                pl.BlockSpec((1, width, out_width), lambda q, source: (q, 0, 0)),
                pl.BlockSpec((owners, rows // owners, out_width), lambda q, source: (0, 0, 0)),
            ],
            scratch_shapes=[
                pltpu.VMEM((rows, out_width), F32),
                pltpu.VMEM((rows, out_width), BF),
                pltpu.VMEM((pairs, cells, out_width), F32),
            ],
        ),
        out_shape=[
            jax.ShapeDtypeStruct((phases, width, out_width), F32),
            jax.ShapeDtypeStruct((owners, rows // owners, out_width), BF),
        ],
        compiler_params=params(60),
        cost_estimate=pl.CostEstimate(
            flops=4 * rows * phases * width * out_width,
            bytes_accessed=6 * phases * width * out_width,
            transcendentals=0,
        ),
        name="tube",
    )(source, *maps, upstream, kernel)


def back_kernel(
    half, total_width, pre_ref, stat_ref, grad_ref, gain_ref, bias_ref, dw_ref,
    scaled_ref, sums_ref, back_ref, mean_ref, rstd_ref, first_ref, second_ref,
):
    step, steps = pl.program_id(0), pl.num_programs(0)
    cells = half * half

    @pl.when(step == 0)
    def _():
        spread_stats(stat_ref[0], total_width, mean_ref, rstd_ref)
        first_ref[...] = jnp.zeros_like(first_ref)
        second_ref[...] = jnp.zeros_like(second_ref)

    taps = load_taps(dw_ref)
    gain = gain_ref[...]
    normed, shifted, sig, _, mixed, around = forward(
        pre_ref[0], mean_ref[...], rstd_ref[...], gain, bias_ref[...], taps, half
    )
    grad_maps, grad_mixed = {}, {}
    for u in range(2):
        for v in range(2):
            value = mixed[u, v]
            gate = sigmoid(value)
            slope = gate * (1.0 + value * (1.0 - gate))
            grad = grad_ref[0, 2 * u + v].astype(F32).reshape(half, half, LANES)
            grad_maps[u, v] = grad
            grad_mixed[u, v] = grad * slope
    for a in (-1, 0, 1):
        for b in (-1, 0, 1):
            total = None
            for u in range(2):
                for v in range(2):
                    part = grad_mixed[u, v] * around[u, v, a, b]
                    total = part if total is None else total + part
            place = 3 * (a + 1) + b + 1
            sums_ref[place : place + 1] = jnp.sum(
                total.reshape(cells, LANES), axis=0, keepdims=True
            )
    spread = neighbours(grad_mixed)
    gain_total, bias_total = None, None
    for u in range(2):
        for v in range(2):
            total = grad_maps[u, v]
            for a in (-1, 0, 1):
                for b in (-1, 0, 1):
                    total = total + taps[a + 1][b + 1] * spread[u, v, -a, -b]
            gate, value = sig[u, v], shifted[u, v]
            grad_shift = total.reshape(cells, LANES) * (gate * (1.0 + value * (1.0 - gate)))
            along = grad_shift * normed[u, v]
            gain_total = along if gain_total is None else gain_total + along
            bias_total = grad_shift if bias_total is None else bias_total + grad_shift
            scaled = grad_shift * gain
            rows = slice((2 * u + v) * cells, (2 * u + v + 1) * cells)
            scaled_ref[rows] = scaled
            first_ref[rows] += scaled
            second_ref[rows] += along * gain
    sums_ref[9:10] = jnp.sum(gain_total, axis=0, keepdims=True)
    sums_ref[10:11] = jnp.sum(bias_total, axis=0, keepdims=True)
    sums_ref[11:16] = jnp.zeros((5, LANES), F32)

    @pl.when(step == steps - 1)
    def _():
        back_ref[...] = columns_to_rows(
            [
                jnp.sum(first_ref[...], axis=1, keepdims=True),
                jnp.sum(second_ref[...], axis=1, keepdims=True),
            ]
        )


def back_call(pre, stats, grad_maps, gain, bias, dw, half):
    _, phases, cells, width = pre.shape
    blocks = stats.shape[1]
    tokens = phases * cells
    row = pl.BlockSpec((1, LANES), lambda c: (0, c))
    block = pl.BlockSpec((1, phases, cells, LANES), lambda c: (0, 0, 0, c))
    return pl.pallas_call(
        functools.partial(back_kernel, half, width),
        grid=(width // LANES,),
        in_specs=[
            block,
            pl.BlockSpec((1, blocks, 8, tokens), lambda c: (0, 0, 0, 0)),
            block,
            row,
            row,
            pl.BlockSpec((9, LANES), lambda c: (0, c)),
        ],
        out_specs=[
            pl.BlockSpec((tokens, LANES), lambda c: (0, c)),
            pl.BlockSpec((16, LANES), lambda c: (0, c)),
            pl.BlockSpec((8, tokens), lambda c: (0, 0)),
        ],
        out_shape=[
            jax.ShapeDtypeStruct((tokens, width), F32),
            jax.ShapeDtypeStruct((16, width), F32),
            jax.ShapeDtypeStruct((8, tokens), F32),
        ],
        scratch_shapes=[pltpu.VMEM((tokens, LANES), F32)] * 4,
        compiler_params=params(8),
        cost_estimate=pl.CostEstimate(
            flops=150 * pre.size, bytes_accessed=10 * pre.size, transcendentals=2 * pre.size
        ),
        name="back",
    )(pre, stats, grad_maps, gain, bias, dw)


def turn_kernel(
    total_width, scaled_ref, pre_ref, stat_ref, back_ref, sums_ref, out_ref, mean_ref, rstd_ref, first_ref, second_ref
):
    tokens, width = scaled_ref.shape
    owners, rows, _ = out_ref.shape
    share = width // owners
    spread_stats(stat_ref[0], total_width, mean_ref, rstd_ref)
    column = rows_to_columns(
        jnp.sum(back_ref[...], axis=0) * (1.0 / (total_width * back_ref.shape[0]))
    )
    first_ref[...] = jnp.broadcast_to(column[0], first_ref.shape)
    second_ref[...] = jnp.broadcast_to(column[1], second_ref.shape)
    mean, rstd, first, second = mean_ref[...], rstd_ref[...], first_ref[...], second_ref[...]
    for part in range(width // LANES):
        lanes = slice(part * LANES, (part + 1) * LANES)
        normed = (pre_ref[0, :, :, lanes].reshape(tokens, LANES) - mean) * rstd
        grad = ((scaled_ref[:, lanes] - first - normed * second) * rstd).T.astype(BF)
        row = part * LANES
        while row < (part + 1) * LANES:
            owner, place = divmod(row, share)
            count = min(share - place, (part + 1) * LANES - row)
            out_ref[owner, place : place + count] = grad[row - part * LANES : row - part * LANES + count]
            row += count
    for owner in range(owners):
        value = sums_ref[:, owner * share : (owner + 1) * share]
        large = value.astype(BF)
        small = (value - large.astype(F32)).astype(BF)
        edge = jnp.zeros((16, LANES - share), BF)
        out_ref[owner, rows - 16 :, :LANES] = jnp.concatenate([large, edge], axis=1)
        out_ref[owner, rows - 16 :, LANES:] = jnp.concatenate([small, edge], axis=1)


def turn_call(scaled, pre, stats, back, sums, owners):
    tokens, width = scaled.shape
    rows = -(-(width // owners) // 16) * 16 + 16
    return pl.pallas_call(
        functools.partial(turn_kernel, width),
        out_shape=jax.ShapeDtypeStruct((owners, rows, tokens), BF),
        scratch_shapes=[pltpu.VMEM((tokens, LANES), F32)] * 4,
        compiler_params=params(10),
        cost_estimate=pl.CostEstimate(
            flops=8 * scaled.size, bytes_accessed=10 * scaled.size, transcendentals=0
        ),
        name="turn",
    )(scaled, pre, stats, back, sums)


def weight_kernel(counts, info_ref, grad_ref, *refs):
    total_pieces = sum(counts)
    pieces = refs[:total_pieces]
    out_ref, dw_ref, gain_ref, bias_ref, rows_ref, held_ref, total_ref, sems = refs[total_pieces:]
    groups, frame = len(counts), grad_ref.shape[2]
    cells = frame // 4
    share = out_ref.shape[0]
    slots = held_ref.shape[0]

    def copies(group):
        first = sum(counts[:group])
        length = frame // counts[group]
        return [
            pltpu.make_async_copy(
                pieces[first + i],
                held_ref.at[group % slots, pl.ds(i * length, length)],
                sems.at[group % slots, i],
            )
            for i in range(counts[group])
        ]

    for group in range(min(slots, groups)):
        for copy in copies(group):
            copy.start()

    own = info_ref[0]
    if share < LANES:
        rows_ref[:, share:] = jnp.zeros((groups, LANES - share, frame), BF)
    for group in range(groups):
        value = grad_ref[info_ref[1 + group], :share].astype(F32)
        if group:
            value = jnp.where((own & 2) == 2, pltpu.roll(value, 2 * cells, 1), value)
            part = lax.broadcasted_iota(jnp.int32, value.shape, 1) // cells
            swapped = jnp.where(
                (part & 1) == 0, pltpu.roll(value, 3 * cells, 1), pltpu.roll(value, cells, 1)
            )
            value = jnp.where((own & 1) == 1, swapped, value)
        rows_ref[group, :share] = value.astype(BF)
    total = jnp.zeros((16, LANES), F32)
    for group in range(groups):
        tail = grad_ref[group, grad_ref.shape[1] - 16 :].astype(F32)
        total = total + tail[:, :LANES] + tail[:, LANES : 2 * LANES]
    for row in range(3):
        dw_ref[row] = total[3 * row : 3 * row + 3, :share]
    gain_ref[...] = total[9:10, :share]
    bias_ref[...] = total[10:11, :share]

    for group in range(groups):
        for copy in copies(group):
            copy.wait()
        value = jnp.dot(rows_ref[group], held_ref[group % slots], preferred_element_type=F32)
        if group == 0:
            total_ref[...] = value
        elif group < groups - 1:
            total_ref[...] += value
        else:
            out_ref[...] = (total_ref[...] + value)[:share]
        if group + slots < groups:
            for copy in copies(group + slots):
                copy.start()


def weight_call(info, groups, grad, share):
    count, rows, tokens = grad.shape
    depth = groups[0][0].shape[1]
    pieces = [piece for group in groups for piece in group]
    slots = min(count, 8)
    return pl.pallas_call(
        functools.partial(weight_kernel, [len(group) for group in groups]),
        in_specs=[
            pl.BlockSpec(memory_space=pltpu.SMEM),
            pl.BlockSpec(memory_space=pltpu.VMEM),
        ]
        + [pl.BlockSpec(memory_space=pl.ANY)] * len(pieces),
        out_specs=[pl.BlockSpec(memory_space=pltpu.VMEM)] * 4,
        out_shape=[
            jax.ShapeDtypeStruct((share, depth), F32),
            jax.ShapeDtypeStruct((3, 3, share), F32),
            jax.ShapeDtypeStruct((1, share), F32),
            jax.ShapeDtypeStruct((1, share), F32),
        ],
        scratch_shapes=[
            pltpu.VMEM((count, LANES, tokens), BF),
            pltpu.VMEM((slots, tokens, depth), BF),
            pltpu.VMEM((LANES, depth), F32),
            pltpu.SemaphoreType.DMA((slots, 4)),
        ],
        compiler_params=params(60),
        cost_estimate=pl.CostEstimate(
            flops=2 * LANES * count * tokens * depth,
            bytes_accessed=2 * count * tokens * depth,
            transcendentals=0,
        ),
        name="weight",
    )(info, grad, *pieces)


def tie(value, *before):
    return lax.optimization_barrier((value, before))[0]


def together(*values):
    return lax.optimization_barrier(values)


def shards(patches, w_in, ln_gain, ln_bias, dw_kernel, w_tube, grad_out, clip_frames, clip_batch):
    ranks, sections, blocks = lax.axis_size("dp"), lax.axis_size("section"), lax.axis_size("mp")
    rank, side, own = lax.axis_index("dp"), lax.axis_index("section"), lax.axis_index("mp")
    grid, depth = patches.shape[2], patches.shape[4]
    half = grid // 2
    cells = half * half
    width = w_in.shape[1]
    out_width = w_tube.shape[4]
    total_pairs = grad_out.shape[0]
    share = width // (ranks * sections)
    gain, bias = ln_gain[None, :], ln_bias[None, :]
    dw = dw_kernel.reshape(9, width)
    kernel = w_tube.reshape(4, width, out_width)
    straight = jnp.arange(4, dtype=jnp.int32)
    order = own ^ straight
    swap = [(i, (i + 1) % sections) for i in range(sections)]
    hops = sorted(range(1, ranks), key=lambda k: (min(k, ranks - k), k))
    source = jnp.stack([rank] + [(rank - k) % ranks for k in hops]).astype(jnp.int32)

    def over_x(value):
        return lax.ppermute(value, "mp", CROSS)

    def over_core(value):
        return lax.ppermute(value, "mp", CORE)

    def over_y(value):
        return lax.ppermute(value, "section", swap)

    def norm_stats(stat):
        return lax.all_gather(stat, "mp", axis=1)

    def over_z(value, hop):
        return lax.ppermute(value, "dp", [(i, (i + hop) % ranks) for i in range(ranks)])

    rows = patches.reshape(grid * grid, depth)
    piece = phase_call(own[None].astype(jnp.int32), rows, 1, half)
    early = over_z(piece, hops[0])
    other = phase_call(own[None].astype(jnp.int32) ^ 2, tie(rows, piece), 1, half)
    across, across_x = [over_y(piece)], [over_y(other)]

    weight = pair_scale(clip_frames, clip_batch, total_pairs, clip_frames.shape[0])
    upstream = (tie(grad_out, piece).astype(F32) * weight[:, None, None]).astype(BF)
    later = tie(piece, upstream)
    fetched = [over_z(later, hop) for hop in hops[1:]]
    term = term_call(upstream.reshape(total_pairs * cells, out_width), kernel, cells)
    phased = phase_call(straight[:1], tie(rows, term), 4, half)
    own_pre, own_stat = pre_call(straight, [[phased]], w_in, cells)
    own_stat = norm_stats(own_stat)
    own_stat, early, across, across_x = together(own_stat, early, across, across_x)
    crossed = [over_x(early)]
    across.append(over_y(early))
    own_maps = maps_call(own_pre, own_stat, gain, bias, dw, half)
    own_maps, term, early, fetched, crossed, across = together(
        own_maps, term, early, fetched, crossed, across
    )

    grad_maps = lax.psum_scatter(term, "dp", scatter_dimension=0, tiled=True)
    crossed += [over_x(value) for value in fetched]
    groups = [[early, over_core(early), crossed[0], over_core(crossed[0])]]
    pre, stat = pre_call(order, groups, w_in, cells)
    pres, stats = [pre], [stat]
    across += [over_y(value) for value in fetched]
    across_x.append(over_y(crossed[0]))
    pres, stats, crossed[1:], fetched, across = together(
        pres, stats, crossed[1:], fetched, across
    )
    across_x += [over_y(value) for value in crossed[1:]]
    groups += [[a, over_core(a), b, over_core(b)] for a, b in zip(fetched, crossed[1:])]
    for start in range(1, ranks - 1, 2):
        pre, stat = pre_call(order, groups[start : start + 2], w_in, cells)
        pres.append(pre)
        stats.append(stat)
    stat = norm_stats(jnp.concatenate(stats, axis=0))
    stat, across_x[1], grad_maps = together(stat, across_x[1], grad_maps)

    scaled, sums, back = back_call(own_pre, own_stat, grad_maps, gain, bias, dw, half)
    back = lax.all_gather(back, "mp", axis=0)
    turned = turn_call(scaled, own_pre, own_stat, back, sums, ranks * sections)
    turned, stat, across, across_x = together(turned, stat, across, across_x)
    received = lax.all_to_all(turned, ("dp", "section"), 0, 0, tiled=True)
    across = [[a, over_core(a), b, over_core(b)] for a, b in zip(across, across_x)]
    maps, start = [own_maps], 0
    for pre in pres:
        part = stat[start : start + pre.shape[0]]
        maps.append(maps_call(pre, part, gain, bias, dw, half))
        start += pre.shape[0]
    grad_w_tube, partial = tube_call(source, maps, upstream, kernel, sections * blocks)
    partial, received, across = together(partial, received, across)
    partial = lax.all_to_all(partial, ("section", "mp"), 0, 0, tiled=True)
    place = jnp.concatenate([source * sections + side, source * sections + (sections - 1 - side)])
    info = jnp.concatenate([own[None], place]).astype(jnp.int32)
    grad_w_in, grad_dw, grad_gain, grad_bias = weight_call(
        info, [[phased]] + groups + across, received, share
    )
    partial, grad_w_in = together(partial, grad_w_in)
    tubes = jnp.sum(partial.astype(F32), axis=0).astype(BF).reshape(total_pairs, -1, out_width)
    return (
        tubes,
        grad_w_in.T,
        grad_gain.reshape(share),
        grad_bias.reshape(share),
        grad_dw,
        grad_w_tube.reshape(w_tube.shape),
    )


def solution(mesh):
    placed = (
        P("dp", "section", None, None, None),
        P(None, "mp"),
        P("mp"),
        P("mp"),
        P(None, None, "mp"),
        P("section", None, None, "mp", "dp"),
        P(None, None, "dp"),
        P(),
        P(),
    )
    return jax.shard_map(
        shards,
        mesh=mesh,
        in_specs=placed,
        out_specs=(
            P(None, ("section", "mp"), "dp"),
            P(None, ("mp", "dp", "section")),
            P(("mp", "dp", "section")),
            P(("mp", "dp", "section")),
            P(None, None, ("mp", "dp", "section")),
            P("section", None, None, "mp", "dp"),
        ),
        check_vma=False,
    )
```

```python
import functools

import jax
import jax.numpy as jnp
from jax import lax
from jax.experimental import pallas as pl
from jax.experimental.pallas import tpu as pltpu
from jax.sharding import PartitionSpec as P

CH = 3584
MICRO = 4
EPS = 1e-06
LANES = 128
BF = jnp.bfloat16
F32 = jnp.float32
CORE = [(0, 1), (1, 0), (2, 3), (3, 2)]
CROSS = [(0, 2), (2, 0), (1, 3), (3, 1)]
TAP = {(u, a): ((u + a) % 2, (u + a) // 2) for u in range(2) for a in (-1, 0, 1)}


def params(mib):
    return pltpu.CompilerParams(vmem_limit_bytes=mib * 2**20)


def pair_scale(clip_frames, clip_batch, count, nclip):
    halves = clip_frames // 2
    ends = jnp.cumsum(halves)
    starts = ends - halves
    places = jnp.arange(count, dtype=jnp.int32)
    member = ((places[:, None] >= starts[None, :]) & (places[:, None] < ends[None, :])).astype(F32)
    batch_hot = (clip_batch[:, None] == jnp.arange(MICRO, dtype=jnp.int32)[None, :]).astype(F32)
    batch_pairs = jnp.sum(batch_hot * halves.astype(F32)[:, None], axis=0)
    clip_load = jnp.sum(batch_hot * batch_pairs[None, :], axis=1)
    clip_scale = 10.0 * nclip / (MICRO * clip_load)
    return jnp.sum(member * clip_scale[None, :], axis=1)


def sigmoid(value):
    return 0.5 + 0.5 * jnp.tanh(0.5 * value)


def columns_to_rows(columns):
    rows = columns[0].shape[0]
    lane = lax.broadcasted_iota(jnp.int32, (rows, LANES), 1)
    wide = jnp.zeros((rows, LANES), F32)
    for place, column in enumerate(columns):
        wide = jnp.where(lane == place, column, wide)
    return wide.T[:8]


def rows_to_columns(stacked):
    padded = jnp.concatenate([stacked, jnp.zeros((LANES - 8, stacked.shape[1]), F32)], axis=0)
    turned = padded.T
    return [turned[:, place : place + 1] for place in range(8)]


def term_kernel(rank_ref, up_ref, w_ref, even_ref, odd_ref, rows_ref):
    half_ranks, _, cells, width = even_ref.shape
    ranks = 2 * half_ranks

    @pl.when(pl.program_id(0) == 0)
    def _():
        for place in range(ranks):
            rows_ref[place * cells : (place + 1) * cells] = up_ref[rank_ref[0] ^ place]

    value = lax.dot_general(
        rows_ref[...], w_ref[0], (((1,), (1,)), ((), ())), preferred_element_type=F32
    ).astype(BF)
    for place in range(ranks):
        out_ref = odd_ref if place % 2 else even_ref
        out_ref[place // 2, 0] = value[place * cells : (place + 1) * cells]


def term_call(rank, upstream, kernel):
    pairs, cells, out_width = upstream.shape
    phases, width, _ = kernel.shape
    block = pl.BlockSpec((pairs // 2, 1, cells, width), lambda q, rank: (0, q, 0, 0))
    return pl.pallas_call(
        term_kernel,
        grid_spec=pltpu.PrefetchScalarGridSpec(
            num_scalar_prefetch=1,
            grid=(phases,),
            in_specs=[
                pl.BlockSpec((pairs, cells, out_width), lambda q, rank: (0, 0, 0)),
                pl.BlockSpec((1, width, out_width), lambda q, rank: (q, 0, 0)),
            ],
            out_specs=[block, block],
            scratch_shapes=[pltpu.VMEM((pairs * cells, out_width), BF)],
        ),
        out_shape=[jax.ShapeDtypeStruct((pairs // 2, phases, cells, width), BF)] * 2,
        compiler_params=params(24),
        cost_estimate=pl.CostEstimate(
            flops=2 * pairs * cells * phases * width * out_width,
            bytes_accessed=2 * phases * width * (out_width + pairs * cells),
            transcendentals=0,
        ),
        name="term",
    )(rank, upstream, kernel)


def phase_rows(shape, first, half):
    row = lax.broadcasted_iota(jnp.int32, shape, 0) + first * half * half
    token = lax.broadcasted_iota(jnp.int32, shape, 1)
    phase, cell = row // (half * half), row % (half * half)
    wanted = 2 * half * (2 * (cell // half) + phase // 2) + 2 * (cell % half) + phase % 2
    return jnp.where(token == wanted, 1.0, 0.0).astype(BF)


def phase_kernel(half, first_ref, rows_ref, out_ref):
    hot = phase_rows((out_ref.shape[0], rows_ref.shape[0]), first_ref[0], half)
    out_ref[...] = jnp.dot(hot, rows_ref[...], preferred_element_type=F32).astype(BF)


def phase_call(first, rows, count, half):
    tokens, depth = rows.shape
    out_rows = count * half * half
    return pl.pallas_call(
        functools.partial(phase_kernel, half),
        grid_spec=pltpu.PrefetchScalarGridSpec(
            num_scalar_prefetch=1,
            grid=(1,),
            in_specs=[pl.BlockSpec((tokens, depth), lambda k, first: (0, 0))],
            out_specs=pl.BlockSpec((out_rows, depth), lambda k, first: (0, 0)),
        ),
        out_shape=jax.ShapeDtypeStruct((out_rows, depth), BF),
        compiler_params=params(12),
        cost_estimate=pl.CostEstimate(
            flops=2 * tokens * out_rows * depth,
            bytes_accessed=2 * depth * (tokens + out_rows),
            transcendentals=0,
        ),
        name="phase",
    )(first, rows)


def pre_kernel(groups, each, order_ref, *refs):
    pieces, (w_ref, pre_ref, stat_ref) = refs[: each * groups], refs[each * groups :]
    width = w_ref.shape[1]
    cells = pre_ref.shape[2]
    frame = 4 * cells
    rows = jnp.concatenate([ref[...] for ref in pieces], axis=0)
    value = jnp.dot(rows, w_ref[...], preferred_element_type=F32)
    for group in range(groups):
        for place in range(4):
            start = group * frame + place * cells
            pre_ref[group, order_ref[place]] = value[start : start + cells]
        part = pre_ref[group].reshape(frame, width)
        mean = jnp.sum(part, axis=1, keepdims=True) * (1.0 / width)
        apart = part - mean
        spread = jnp.sum(apart * apart, axis=1, keepdims=True)
        stat_ref[group] = columns_to_rows([mean, spread])


def pre_call(order, groups, w_in, cells):
    depth, width = w_in.shape
    count, each = len(groups), len(groups[0])
    pieces = [piece for group in groups for piece in group]
    return pl.pallas_call(
        functools.partial(pre_kernel, count, each),
        grid_spec=pltpu.PrefetchScalarGridSpec(
            num_scalar_prefetch=1,
            grid=(),
            in_specs=[pl.BlockSpec(memory_space=pltpu.VMEM)] * (len(pieces) + 1),
            out_specs=[pl.BlockSpec(memory_space=pltpu.VMEM)] * 2,
        ),
        out_shape=[
            jax.ShapeDtypeStruct((count, 4, cells, width), F32),
            jax.ShapeDtypeStruct((count, 8, 4 * cells), F32),
        ],
        compiler_params=params(12),
        cost_estimate=pl.CostEstimate(
            flops=8 * count * cells * depth * width,
            bytes_accessed=2 * depth * (width + 4 * count * cells),
            transcendentals=0,
        ),
        name="pre",
    )(order, *pieces, w_in)


def spread_stats(stats, width, mean_ref, rstd_ref):
    blocks = stats.shape[0]
    means, spreads = stats[:, 0], stats[:, 1]
    mean = jnp.sum(means, axis=0, keepdims=True) * (1.0 / blocks)
    apart = means - mean
    total = jnp.sum(spreads, axis=0, keepdims=True) + width * jnp.sum(
        apart * apart, axis=0, keepdims=True
    )
    rstd = lax.rsqrt(total * (1.0 / (width * blocks)) + EPS)
    row = lax.broadcasted_iota(jnp.int32, (8, mean.shape[1]), 0)
    column = rows_to_columns(jnp.where(row == 0, mean, jnp.where(row == 1, rstd, 0.0)))
    mean_ref[...] = jnp.broadcast_to(column[0], mean_ref.shape)
    rstd_ref[...] = jnp.broadcast_to(column[1], rstd_ref.shape)


def shift_rows(value, by):
    if by == 0:
        return value
    empty = jnp.zeros_like(value[:1])
    if by < 0:
        return jnp.concatenate([empty, value[:-1]], axis=0)
    return jnp.concatenate([value[1:], empty], axis=0)


def shift_columns(value, by):
    if by == 0:
        return value
    half = value.shape[1]
    place = lax.broadcasted_iota(jnp.int32, value.shape, 1)
    if by < 0:
        return jnp.where(place == 0, 0.0, pltpu.roll(value, 1, 1))
    return jnp.where(place == half - 1, 0.0, pltpu.roll(value, half - 1, 1))


def neighbours(grid_values):
    sides = {}
    for u in range(2):
        for v in range(2):
            for by in (0, -1 if v == 1 else 1):
                sides[u, v, by] = shift_columns(grid_values[u, v], by)
    found = {}
    for u in range(2):
        for v in range(2):
            for a in (-1, 0, 1):
                for b in (-1, 0, 1):
                    row, by_row = TAP[u, a]
                    column, by_column = TAP[v, b]
                    found[u, v, a, b] = shift_rows(sides[row, column, by_column], by_row)
    return found


def forward(pre, mean, rstd, gain, bias, taps, half):
    cells = half * half
    normed, shifted, sig, act, mixed = {}, {}, {}, {}, {}
    for u in range(2):
        for v in range(2):
            place = 2 * u + v
            rows = slice(place * cells, (place + 1) * cells)
            value = (pre[place] - mean[rows]) * rstd[rows]
            moved = value * gain + bias
            gate = sigmoid(moved)
            normed[u, v], shifted[u, v], sig[u, v] = value, moved, gate
            act[u, v] = (moved * gate).reshape(half, half, LANES)
    around = neighbours(act)
    for u in range(2):
        for v in range(2):
            total = None
            for a in (-1, 0, 1):
                for b in (-1, 0, 1):
                    part = taps[a + 1][b + 1] * around[u, v, a, b]
                    total = part if total is None else total + part
            mixed[u, v] = total
    return normed, shifted, sig, act, mixed, around


def load_taps(dw_ref):
    return [[dw_ref[3 * a + b : 3 * a + b + 1] for b in range(3)] for a in range(3)]


def maps_kernel(half, total_width, pre_ref, stat_ref, gain_ref, bias_ref, dw_ref, maps_ref, mean_ref, rstd_ref):
    cells = half * half

    @pl.when(pl.program_id(1) == 0)
    def _():
        spread_stats(stat_ref[0], total_width, mean_ref, rstd_ref)

    _, _, _, act, mixed, _ = forward(
        pre_ref[0], mean_ref[...], rstd_ref[...], gain_ref[...], bias_ref[...], load_taps(dw_ref), half
    )
    for u in range(2):
        for v in range(2):
            value = mixed[u, v]
            maps = act[u, v] + value * sigmoid(value)
            maps_ref[0, 2 * u + v] = maps.reshape(cells, LANES).astype(BF)


def maps_call(pre, stats, gain, bias, dw, half):
    count, phases, cells, width = pre.shape
    blocks = stats.shape[1]
    row = pl.BlockSpec((1, LANES), lambda p, c: (0, c))
    block = pl.BlockSpec((1, phases, cells, LANES), lambda p, c: (p, 0, 0, c))
    return pl.pallas_call(
        functools.partial(maps_kernel, half, width),
        grid=(count, width // LANES),
        in_specs=[
            block,
            pl.BlockSpec((1, blocks, 8, phases * cells), lambda p, c: (p, 0, 0, 0)),
            row,
            row,
            pl.BlockSpec((9, LANES), lambda p, c: (0, c)),
        ],
        out_specs=block,
        out_shape=jax.ShapeDtypeStruct(pre.shape, BF),
        scratch_shapes=[pltpu.VMEM((phases * cells, LANES), F32)] * 2,
        compiler_params=params(8),
        cost_estimate=pl.CostEstimate(
            flops=60 * pre.size,
            bytes_accessed=6 * pre.size,
            transcendentals=0,
        ),
        name="maps",
    )(pre, stats, gain, bias, dw)


def tube_kernel(count, source_ref, up_ref, *refs):
    maps_refs = refs[:count]
    w_ref, grad_ref, part_ref, held_ref, w_held, out_held, total_ref, near_ref, sorted_ref, sems = refs[count:]
    pairs, phases, cells, width = held_ref.shape

    copies, start = [], 0
    for place, ref in enumerate(maps_refs):
        copies.append(
            pltpu.make_async_copy(ref, held_ref.at[pl.ds(start, ref.shape[0])], sems.at[0, place])
        )
        start += ref.shape[0]
    loads = [pltpu.make_async_copy(w_ref.at[q], w_held.at[q], sems.at[1, q]) for q in range(phases)]
    stores = [
        pltpu.make_async_copy(out_held.at[q % 2], grad_ref.at[q], sems.at[2, q]) for q in range(phases)
    ]
    for copy in copies + loads:
        copy.start()
    for pair in range(pairs):
        near_ref[pair * cells : (pair + 1) * cells] = up_ref[source_ref[pair]]
    for copy in copies:
        copy.wait()
    for q in range(phases):
        rows = held_ref[:, q].reshape(pairs * cells, width)
        if q >= 2:
            stores[q - 2].wait()
        out_held[q % 2] = lax.dot_general(
            rows, near_ref[...], (((0,), (0,)), ((), ())), preferred_element_type=F32
        )
        stores[q].start()
        loads[q].wait()
        value = jnp.dot(rows, w_held[q], preferred_element_type=F32)
        if q == 0:
            total_ref[...] = value
        else:
            total_ref[...] += value
    for pair in range(pairs):
        sorted_ref[source_ref[pair]] = total_ref[pair * cells : (pair + 1) * cells]
    owners = part_ref.shape[0]
    held = cells // owners
    for owner in range(owners):
        part_ref[owner] = jnp.concatenate(
            [sorted_ref[pair, owner * held : (owner + 1) * held] for pair in range(pairs)], axis=0
        ).astype(BF)
    for copy in stores[-2:]:
        copy.wait()


def tube_call(source, maps, upstream, kernel, owners):
    phases, cells, width = maps[0].shape[1:]
    pairs, _, out_width = upstream.shape
    rows = pairs * cells
    return pl.pallas_call(
        functools.partial(tube_kernel, len(maps)),
        in_specs=[pl.BlockSpec(memory_space=pltpu.SMEM), pl.BlockSpec(memory_space=pltpu.VMEM)]
        + [pl.BlockSpec(memory_space=pl.ANY)] * (len(maps) + 1),
        out_specs=[
            pl.BlockSpec(memory_space=pl.ANY),
            pl.BlockSpec(memory_space=pltpu.VMEM),
        ],
        out_shape=[
            jax.ShapeDtypeStruct((phases, width, out_width), F32),
            jax.ShapeDtypeStruct((owners, rows // owners, out_width), BF),
        ],
        scratch_shapes=[
            pltpu.VMEM((pairs, phases, cells, width), BF),
            pltpu.VMEM((phases, width, out_width), BF),
            pltpu.VMEM((2, width, out_width), F32),
            pltpu.VMEM((rows, out_width), F32),
            pltpu.VMEM((rows, out_width), BF),
            pltpu.VMEM((pairs, cells, out_width), F32),
            pltpu.SemaphoreType.DMA((3, max(phases, len(maps)))),
        ],
        compiler_params=params(58),
        cost_estimate=pl.CostEstimate(
            flops=4 * rows * phases * width * out_width,
            bytes_accessed=6 * phases * width * out_width,
            transcendentals=0,
        ),
        name="tube",
    )(source, upstream, *maps, kernel)


def back_kernel(half, total_width, count, pre_ref, stat_ref, gain_ref, bias_ref, dw_ref, *refs):
    grad_refs = refs[:count]
    scaled_ref, sums_ref, back_ref, mean_ref, rstd_ref, first_ref, second_ref = refs[count:]
    step, steps = pl.program_id(0), pl.num_programs(0)
    cells = half * half

    @pl.when(step == 0)
    def _():
        spread_stats(stat_ref[0], total_width, mean_ref, rstd_ref)
        first_ref[...] = jnp.zeros_like(first_ref)
        second_ref[...] = jnp.zeros_like(second_ref)

    taps = load_taps(dw_ref)
    gain = gain_ref[...]
    normed, shifted, sig, _, mixed, around = forward(
        pre_ref[0], mean_ref[...], rstd_ref[...], gain, bias_ref[...], taps, half
    )
    grad_maps, grad_mixed = {}, {}
    for u in range(2):
        for v in range(2):
            value = mixed[u, v]
            gate = sigmoid(value)
            slope = gate * (1.0 + value * (1.0 - gate))
            grad = grad_refs[0][0, 2 * u + v].astype(F32)
            for ref in grad_refs[1:]:
                grad = grad + ref[0, 2 * u + v].astype(F32)
            grad = grad.reshape(half, half, LANES)
            grad_maps[u, v] = grad
            grad_mixed[u, v] = grad * slope
    for a in (-1, 0, 1):
        for b in (-1, 0, 1):
            total = None
            for u in range(2):
                for v in range(2):
                    part = grad_mixed[u, v] * around[u, v, a, b]
                    total = part if total is None else total + part
            place = 3 * (a + 1) + b + 1
            sums_ref[place : place + 1] = jnp.sum(
                total.reshape(cells, LANES), axis=0, keepdims=True
            )
    spread = neighbours(grad_mixed)
    gain_total, bias_total = None, None
    for u in range(2):
        for v in range(2):
            total = grad_maps[u, v]
            for a in (-1, 0, 1):
                for b in (-1, 0, 1):
                    total = total + taps[a + 1][b + 1] * spread[u, v, -a, -b]
            gate, value = sig[u, v], shifted[u, v]
            grad_shift = total.reshape(cells, LANES) * (gate * (1.0 + value * (1.0 - gate)))
            along = grad_shift * normed[u, v]
            gain_total = along if gain_total is None else gain_total + along
            bias_total = grad_shift if bias_total is None else bias_total + grad_shift
            scaled = grad_shift * gain
            rows = slice((2 * u + v) * cells, (2 * u + v + 1) * cells)
            scaled_ref[rows] = scaled
            first_ref[rows] += scaled
            second_ref[rows] += along * gain
    sums_ref[9:10] = jnp.sum(gain_total, axis=0, keepdims=True)
    sums_ref[10:11] = jnp.sum(bias_total, axis=0, keepdims=True)
    sums_ref[11:16] = jnp.zeros((5, LANES), F32)

    @pl.when(step == steps - 1)
    def _():
        back_ref[...] = columns_to_rows(
            [
                jnp.sum(first_ref[...], axis=1, keepdims=True),
                jnp.sum(second_ref[...], axis=1, keepdims=True),
            ]
        )


def back_call(pre, stats, grad_maps, gain, bias, dw, half):
    _, phases, cells, width = pre.shape
    blocks = stats.shape[1]
    tokens = phases * cells
    row = pl.BlockSpec((1, LANES), lambda c: (0, c))
    block = pl.BlockSpec((1, phases, cells, LANES), lambda c: (0, 0, 0, c))
    return pl.pallas_call(
        functools.partial(back_kernel, half, width, len(grad_maps)),
        grid=(width // LANES,),
        in_specs=[
            block,
            pl.BlockSpec((1, blocks, 8, tokens), lambda c: (0, 0, 0, 0)),
            row,
            row,
            pl.BlockSpec((9, LANES), lambda c: (0, c)),
        ]
        + [block] * len(grad_maps),
        out_specs=[
            pl.BlockSpec((tokens, LANES), lambda c: (0, c)),
            pl.BlockSpec((16, LANES), lambda c: (0, c)),
            pl.BlockSpec((8, tokens), lambda c: (0, 0)),
        ],
        out_shape=[
            jax.ShapeDtypeStruct((tokens, width), F32),
            jax.ShapeDtypeStruct((16, width), F32),
            jax.ShapeDtypeStruct((8, tokens), F32),
        ],
        scratch_shapes=[pltpu.VMEM((tokens, LANES), F32)] * 4,
        compiler_params=params(8),
        cost_estimate=pl.CostEstimate(
            flops=150 * pre.size,
            bytes_accessed=10 * pre.size,
            transcendentals=0,
        ),
        name="back",
    )(pre, stats, gain, bias, dw, *grad_maps)


def turn_kernel(
    total_width, scaled_ref, pre_ref, stat_ref, back_ref, sums_ref, out_ref, mean_ref, rstd_ref, first_ref, second_ref
):
    tokens, width = scaled_ref.shape
    owners, rows, _ = out_ref.shape
    share = width // owners
    spread_stats(stat_ref[0], total_width, mean_ref, rstd_ref)
    column = rows_to_columns(
        jnp.sum(back_ref[...], axis=0) * (1.0 / (total_width * back_ref.shape[0]))
    )
    first_ref[...] = jnp.broadcast_to(column[0], first_ref.shape)
    second_ref[...] = jnp.broadcast_to(column[1], second_ref.shape)
    mean, rstd, first, second = mean_ref[...], rstd_ref[...], first_ref[...], second_ref[...]
    for part in range(width // LANES):
        lanes = slice(part * LANES, (part + 1) * LANES)
        normed = (pre_ref[0, :, :, lanes].reshape(tokens, LANES) - mean) * rstd
        grad = ((scaled_ref[:, lanes] - first - normed * second) * rstd).T.astype(BF)
        row = part * LANES
        while row < (part + 1) * LANES:
            owner, place = divmod(row, share)
            count = min(share - place, (part + 1) * LANES - row)
            out_ref[owner, place : place + count] = grad[row - part * LANES : row - part * LANES + count]
            row += count
    for owner in range(owners):
        if rows - 16 > share:
            out_ref[owner, share : rows - 16] = jnp.zeros((rows - 16 - share, tokens), BF)
        value = sums_ref[:, owner * share : (owner + 1) * share]
        large = value.astype(BF)
        small = (value - large.astype(F32)).astype(BF)
        edge = jnp.zeros((16, LANES - share), BF)
        out_ref[owner, rows - 16 :, :LANES] = jnp.concatenate([large, edge], axis=1)
        out_ref[owner, rows - 16 :, LANES:] = jnp.concatenate([small, edge], axis=1)


def turn_call(scaled, pre, stats, back, sums, owners):
    tokens, width = scaled.shape
    rows = -(-(width // owners) // 16) * 16 + 16
    return pl.pallas_call(
        functools.partial(turn_kernel, width),
        out_shape=jax.ShapeDtypeStruct((owners, rows, tokens), BF),
        scratch_shapes=[pltpu.VMEM((tokens, LANES), F32)] * 4,
        compiler_params=params(10),
        cost_estimate=pl.CostEstimate(
            flops=8 * scaled.size,
            bytes_accessed=10 * scaled.size,
            transcendentals=0,
        ),
        name="turn",
    )(scaled, pre, stats, back, sums)


def weight_kernel(counts, info_ref, grad_ref, *refs):
    total_pieces = sum(counts)
    pieces = refs[:total_pieces]
    out_ref, dw_ref, gain_ref, bias_ref, rows_ref, held_ref, total_ref, sems = refs[total_pieces:]
    groups, frame = len(counts), grad_ref.shape[2]
    cells = frame // 4
    share = out_ref.shape[0]
    slots = held_ref.shape[0]

    def copies(group):
        first = sum(counts[:group])
        length = frame // counts[group]
        return [
            pltpu.make_async_copy(
                pieces[first + i],
                held_ref.at[group % slots, pl.ds(i * length, length)],
                sems.at[group % slots, i],
            )
            for i in range(counts[group])
        ]

    for group in range(min(slots, groups)):
        for copy in copies(group):
            copy.start()

    own = info_ref[0]
    if share < LANES:
        rows_ref[:, share:] = jnp.zeros((groups, LANES - share, frame), BF)
    for group in range(groups):
        value = grad_ref[info_ref[1 + group], :share].astype(F32)
        if group:
            value = jnp.where((own & 2) == 2, pltpu.roll(value, 2 * cells, 1), value)
            part = lax.broadcasted_iota(jnp.int32, value.shape, 1) // cells
            swapped = jnp.where(
                (part & 1) == 0, pltpu.roll(value, 3 * cells, 1), pltpu.roll(value, cells, 1)
            )
            value = jnp.where((own & 1) == 1, swapped, value)
        rows_ref[group, :share] = value.astype(BF)
    total = jnp.zeros((16, LANES), F32)
    for group in range(groups):
        tail = grad_ref[group, grad_ref.shape[1] - 16 :].astype(F32)
        total = total + tail[:, :LANES] + tail[:, LANES : 2 * LANES]
    for row in range(3):
        dw_ref[row] = total[3 * row : 3 * row + 3, :share]
    gain_ref[...] = total[9:10, :share]
    bias_ref[...] = total[10:11, :share]

    for group in range(groups):
        for copy in copies(group):
            copy.wait()
        value = jnp.dot(rows_ref[group], held_ref[group % slots], preferred_element_type=F32)
        if group == 0:
            total_ref[...] = value
        elif group < groups - 1:
            total_ref[...] += value
        else:
            out_ref[...] = (total_ref[...] + value)[:share]
        if group + slots < groups:
            for copy in copies(group + slots):
                copy.start()


def weight_call(info, groups, grad, share):
    count, rows, tokens = grad.shape
    depth = groups[0][0].shape[1]
    pieces = [piece for group in groups for piece in group]
    slots = min(count, 8)
    return pl.pallas_call(
        functools.partial(weight_kernel, [len(group) for group in groups]),
        in_specs=[
            pl.BlockSpec(memory_space=pltpu.SMEM),
            pl.BlockSpec(memory_space=pltpu.VMEM),
        ]
        + [pl.BlockSpec(memory_space=pl.ANY)] * len(pieces),
        out_specs=[pl.BlockSpec(memory_space=pltpu.VMEM)] * 4,
        out_shape=[
            jax.ShapeDtypeStruct((share, depth), F32),
            jax.ShapeDtypeStruct((3, 3, share), F32),
            jax.ShapeDtypeStruct((1, share), F32),
            jax.ShapeDtypeStruct((1, share), F32),
        ],
        scratch_shapes=[
            pltpu.VMEM((count, LANES, tokens), BF),
            pltpu.VMEM((slots, tokens, depth), BF),
            pltpu.VMEM((LANES, depth), F32),
            pltpu.SemaphoreType.DMA((slots, 4)),
        ],
        compiler_params=params(60),
        cost_estimate=pl.CostEstimate(
            flops=2 * LANES * count * tokens * depth,
            bytes_accessed=2 * count * tokens * depth,
            transcendentals=0,
        ),
        name="weight",
    )(info, grad, *pieces)


def tie(value, *before):
    return lax.optimization_barrier((value, before))[0]


def together(*values):
    return lax.optimization_barrier(values)


def shards(patches, w_in, ln_gain, ln_bias, dw_kernel, w_tube, grad_out, clip_frames, clip_batch):
    ranks, sections, blocks = lax.axis_size("dp"), lax.axis_size("section"), lax.axis_size("mp")
    rank, side, own = lax.axis_index("dp"), lax.axis_index("section"), lax.axis_index("mp")
    grid, depth = patches.shape[2], patches.shape[4]
    half = grid // 2
    cells = half * half
    width = w_in.shape[1]
    out_width = w_tube.shape[4]
    total_pairs = grad_out.shape[0]
    share = width // (ranks * sections)
    gain, bias = ln_gain[None, :], ln_bias[None, :]
    dw = dw_kernel.reshape(9, width)
    kernel = w_tube.reshape(4, width, out_width)
    straight = jnp.arange(4, dtype=jnp.int32)
    order = own ^ straight
    swap = [(i, (i + 1) % sections) for i in range(sections)]
    source = (rank ^ jnp.arange(ranks, dtype=jnp.int32)).astype(jnp.int32)

    def over_x(value):
        return lax.ppermute(value, "mp", CROSS)

    def over_core(value):
        return lax.ppermute(value, "mp", CORE)

    def over_y(value):
        return lax.ppermute(value, "section", swap)

    def norm_stats(stat):
        return lax.all_gather(stat, "mp", axis=1)

    def over_z(value, mask):
        return lax.ppermute(value, "dp", [(i, i ^ mask) for i in range(ranks)])

    rows = patches.reshape(grid * grid, depth)
    piece = phase_call(own[None].astype(jnp.int32), rows, 1, half)
    early = over_z(piece, 1)
    other = phase_call(own[None].astype(jnp.int32) ^ 2, tie(rows, piece), 1, half)
    across, across_x = [over_y(piece)], [over_y(other)]

    weight = pair_scale(clip_frames, clip_batch, total_pairs, clip_frames.shape[0])
    upstream = (tie(grad_out, piece).astype(F32) * weight[:, None, None]).astype(BF)
    later = tie(piece, upstream)
    fetched = [over_z(later, mask) for mask in range(2, ranks)]
    even, odd = term_call(rank[None].astype(jnp.int32), upstream, kernel)
    phased = phase_call(straight[:1], tie(rows, even), 4, half)
    own_pre, own_stat = pre_call(straight, [[phased]], w_in, cells)
    own_stat = norm_stats(own_stat)
    own_stat, early, across, across_x, odd = together(own_stat, early, across, across_x, odd)
    taken = over_z(odd, 1)
    crossed = [over_x(early)]
    across.append(over_y(early))
    own_maps = maps_call(own_pre, own_stat, gain, bias, dw, half)
    own_maps, early, fetched, crossed, across = together(
        own_maps, early, fetched, crossed, across
    )

    crossed += [over_x(value) for value in fetched]
    groups = [[early, over_core(early), crossed[0], over_core(crossed[0])]]
    pre, stat = pre_call(order, groups, w_in, cells)
    pre, stat, taken = together(pre, stat, taken)
    pres, stats = [pre], [stat]
    grad_maps, rest, step = [even], even[1:], 2
    while step < ranks:
        grad_maps.append(taken)
        rest = (rest.astype(F32) + taken[1:].astype(F32)).astype(BF)
        taken = over_z(rest[::2], step)
        rest = rest[1::2]
        step *= 2
    grad_maps.append(taken)
    across += [over_y(value) for value in fetched]
    across_x.append(over_y(crossed[0]))
    pres, stats, crossed[1:], fetched, across = together(
        pres, stats, crossed[1:], fetched, across
    )
    across_x += [over_y(value) for value in crossed[1:]]
    groups += [[a, over_core(a), b, over_core(b)] for a, b in zip(fetched, crossed[1:])]
    for start in range(1, ranks - 1, 2):
        pre, stat = pre_call(order, groups[start : start + 2], w_in, cells)
        pres.append(pre)
        stats.append(stat)
    stat = norm_stats(jnp.concatenate(stats, axis=0))
    stat, across_x[1], grad_maps = together(stat, across_x[1], grad_maps)

    scaled, sums, back = back_call(own_pre, own_stat, grad_maps, gain, bias, dw, half)
    back = lax.all_gather(back, "mp", axis=0)
    turned = turn_call(scaled, own_pre, own_stat, back, sums, ranks * sections)
    turned, stat, across, across_x = together(turned, stat, across, across_x)
    received = lax.all_to_all(turned, ("dp", "section"), 0, 0, tiled=True)
    across = [[a, over_core(a), b, over_core(b)] for a, b in zip(across, across_x)]
    maps, start = [own_maps], 0
    for pre in pres:
        part = stat[start : start + pre.shape[0]]
        maps.append(maps_call(pre, part, gain, bias, dw, half))
        start += pre.shape[0]
    grad_w_tube, partial = tube_call(source, maps, upstream, kernel, sections * blocks)
    partial, received, across = together(partial, received, across)
    partial = lax.all_to_all(partial, ("section", "mp"), 0, 0, tiled=True)
    place = jnp.concatenate([source * sections + side, source * sections + (sections - 1 - side)])
    info = jnp.concatenate([own[None], place]).astype(jnp.int32)
    grad_w_in, grad_dw, grad_gain, grad_bias = weight_call(
        info, [[phased]] + groups + across, received, share
    )
    partial, grad_w_in = together(partial, grad_w_in)
    tubes = jnp.sum(partial.astype(F32), axis=0).astype(BF).reshape(total_pairs, -1, out_width)
    return (
        tubes,
        grad_w_in.T,
        grad_gain.reshape(share),
        grad_bias.reshape(share),
        grad_dw,
        grad_w_tube.reshape(w_tube.shape),
    )


def solution(mesh):
    placed = (
        P("dp", "section", None, None, None),
        P(None, "mp"),
        P("mp"),
        P("mp"),
        P(None, None, "mp"),
        P("section", None, None, "mp", "dp"),
        P(None, None, "dp"),
        P(),
        P(),
    )
    return jax.shard_map(
        shards,
        mesh=mesh,
        in_specs=placed,
        out_specs=(
            P(None, ("section", "mp"), "dp"),
            P(None, ("mp", "dp", "section")),
            P(("mp", "dp", "section")),
            P(("mp", "dp", "section")),
            P(None, None, ("mp", "dp", "section")),
            P("section", None, None, "mp", "dp"),
        ),
        check_vma=False,
    )
```

```python
import functools

import jax
import jax.numpy as jnp
from jax import lax
from jax.experimental import pallas as pl
from jax.experimental.pallas import tpu as pltpu
from jax.sharding import PartitionSpec as P

CH = 3584
MICRO = 4
EPS = 1e-06
SMALL = pl.CostEstimate(flops=1, bytes_accessed=1, transcendentals=0)
LANES = 128
BF = jnp.bfloat16
F32 = jnp.float32
CORE = [(0, 1), (1, 0), (2, 3), (3, 2)]
CROSS = [(0, 2), (2, 0), (1, 3), (3, 1)]
TAP = {(u, a): ((u + a) % 2, (u + a) // 2) for u in range(2) for a in (-1, 0, 1)}


def params(mib):
    return pltpu.CompilerParams(vmem_limit_bytes=mib * 2**20)


def pair_scale(clip_frames, clip_batch, count, nclip):
    halves = clip_frames // 2
    ends = jnp.cumsum(halves)
    starts = ends - halves
    places = jnp.arange(count, dtype=jnp.int32)
    member = ((places[:, None] >= starts[None, :]) & (places[:, None] < ends[None, :])).astype(F32)
    batch_hot = (clip_batch[:, None] == jnp.arange(MICRO, dtype=jnp.int32)[None, :]).astype(F32)
    batch_pairs = jnp.sum(batch_hot * halves.astype(F32)[:, None], axis=0)
    clip_load = jnp.sum(batch_hot * batch_pairs[None, :], axis=1)
    clip_scale = 10.0 * nclip / (MICRO * clip_load)
    return jnp.sum(member * clip_scale[None, :], axis=1)


def sigmoid(value):
    return 0.5 + 0.5 * jnp.tanh(0.5 * value)


def columns_to_rows(columns):
    rows = columns[0].shape[0]
    lane = lax.broadcasted_iota(jnp.int32, (rows, LANES), 1)
    wide = jnp.zeros((rows, LANES), F32)
    for place, column in enumerate(columns):
        wide = jnp.where(lane == place, column, wide)
    return wide.T[:8]


def rows_to_columns(stacked):
    padded = jnp.concatenate([stacked, jnp.zeros((LANES - 8, stacked.shape[1]), F32)], axis=0)
    turned = padded.T
    return [turned[:, place : place + 1] for place in range(8)]


def term_kernel(rank_ref, up_ref, w_ref, even_ref, odd_ref, rows_ref):
    half_ranks, _, cells, width = even_ref.shape
    ranks = 2 * half_ranks

    @pl.when(pl.program_id(0) == 0)
    def _():
        for place in range(ranks):
            rows_ref[place * cells : (place + 1) * cells] = up_ref[rank_ref[0] ^ place]

    value = lax.dot_general(
        rows_ref[...], w_ref[0], (((1,), (1,)), ((), ())), preferred_element_type=F32
    ).astype(BF)
    for place in range(ranks):
        out_ref = odd_ref if place % 2 else even_ref
        out_ref[place // 2, 0] = value[place * cells : (place + 1) * cells]


def term_call(rank, upstream, kernel):
    pairs, cells, out_width = upstream.shape
    phases, width, _ = kernel.shape
    block = pl.BlockSpec((pairs // 2, 1, cells, width), lambda q, rank: (0, q, 0, 0))
    return pl.pallas_call(
        term_kernel,
        grid_spec=pltpu.PrefetchScalarGridSpec(
            num_scalar_prefetch=1,
            grid=(phases,),
            in_specs=[
                pl.BlockSpec((pairs, cells, out_width), lambda q, rank: (0, 0, 0)),
                pl.BlockSpec((1, width, out_width), lambda q, rank: (q, 0, 0)),
            ],
            out_specs=[block, block],
            scratch_shapes=[pltpu.VMEM((pairs * cells, out_width), BF)],
        ),
        out_shape=[jax.ShapeDtypeStruct((pairs // 2, phases, cells, width), BF)] * 2,
        compiler_params=params(24),
        cost_estimate=pl.CostEstimate(
            flops=2 * pairs * cells * phases * width * out_width,
            bytes_accessed=2 * phases * width * (out_width + pairs * cells),
            transcendentals=0,
        ),
        name="term",
    )(rank, upstream, kernel)


def phase_rows(shape, first, half):
    row = lax.broadcasted_iota(jnp.int32, shape, 0) + first * half * half
    token = lax.broadcasted_iota(jnp.int32, shape, 1)
    phase, cell = row // (half * half), row % (half * half)
    wanted = 2 * half * (2 * (cell // half) + phase // 2) + 2 * (cell % half) + phase % 2
    return jnp.where(token == wanted, 1.0, 0.0).astype(BF)


def phase_kernel(half, first_ref, rows_ref, out_ref):
    hot = phase_rows((out_ref.shape[0], rows_ref.shape[0]), first_ref[0], half)
    out_ref[...] = jnp.dot(hot, rows_ref[...], preferred_element_type=F32).astype(BF)


def phase_call(first, rows, count, half):
    tokens, depth = rows.shape
    out_rows = count * half * half
    return pl.pallas_call(
        functools.partial(phase_kernel, half),
        grid_spec=pltpu.PrefetchScalarGridSpec(
            num_scalar_prefetch=1,
            grid=(1,),
            in_specs=[pl.BlockSpec((tokens, depth), lambda k, first: (0, 0))],
            out_specs=pl.BlockSpec((out_rows, depth), lambda k, first: (0, 0)),
        ),
        out_shape=jax.ShapeDtypeStruct((out_rows, depth), BF),
        compiler_params=params(12),
        cost_estimate=pl.CostEstimate(
            flops=2 * tokens * out_rows * depth,
            bytes_accessed=2 * depth * (tokens + out_rows),
            transcendentals=0,
        ),
        name="phase",
    )(first, rows)


def pre_kernel(groups, cuts, order_ref, *refs):
    pieces, (w_ref, pre_ref, stat_ref, held_ref, total_ref, sems) = refs[:-6], refs[-6:]
    width = w_ref.shape[1]
    cells = pre_ref.shape[2]
    frame = 4 * cells
    parts = [slice(low, high) for low, high in zip(cuts[:-1], cuts[1:])]
    copies = [
        pltpu.make_async_copy(w_ref.at[part], held_ref.at[part], sems.at[place])
        for place, part in enumerate(parts)
    ]
    for copy in copies:
        copy.start()
    for place, part in enumerate(parts):
        copies[place].wait()
        rows = jnp.concatenate([ref[:, part] for ref in pieces], axis=0)
        value = jnp.dot(rows, held_ref[part], preferred_element_type=F32)
        if place == 0:
            total_ref[...] = value
        elif place < len(parts) - 1:
            total_ref[...] += value
    value = total_ref[...] + value
    for group in range(groups):
        for place in range(4):
            start = group * frame + place * cells
            pre_ref[group, order_ref[place]] = value[start : start + cells]
        part = pre_ref[group].reshape(frame, width)
        mean = jnp.sum(part, axis=1, keepdims=True) * (1.0 / width)
        apart = part - mean
        spread = jnp.sum(apart * apart, axis=1, keepdims=True)
        stat_ref[group] = columns_to_rows([mean, spread])


def pre_call(order, groups, w_in, cells):
    depth, width = w_in.shape
    count = len(groups)
    pieces = [piece for group in groups for piece in group]
    quarter = -(-depth // 1024) * 256
    cuts = list(range(0, depth - quarter // 2, quarter)) + [depth]
    return pl.pallas_call(
        functools.partial(pre_kernel, count, cuts),
        grid_spec=pltpu.PrefetchScalarGridSpec(
            num_scalar_prefetch=1,
            grid=(),
            in_specs=[pl.BlockSpec(memory_space=pltpu.VMEM)] * len(pieces)
            + [pl.BlockSpec(memory_space=pltpu.HBM)],
            out_specs=[pl.BlockSpec(memory_space=pltpu.VMEM)] * 2,
            scratch_shapes=[
                pltpu.VMEM((depth, width), BF),
                pltpu.VMEM((4 * count * cells, width), F32),
                pltpu.SemaphoreType.DMA((len(cuts) - 1,)),
            ],
        ),
        out_shape=[
            jax.ShapeDtypeStruct((count, 4, cells, width), F32),
            jax.ShapeDtypeStruct((count, 8, 4 * cells), F32),
        ],
        compiler_params=params(24),
        cost_estimate=SMALL,
        name="pre",
    )(order, *pieces, w_in)


def spread_stats(stats, width, mean_ref, rstd_ref):
    blocks = stats.shape[0]
    means, spreads = stats[:, 0], stats[:, 1]
    mean = jnp.sum(means, axis=0, keepdims=True) * (1.0 / blocks)
    apart = means - mean
    total = jnp.sum(spreads, axis=0, keepdims=True) + width * jnp.sum(
        apart * apart, axis=0, keepdims=True
    )
    rstd = lax.rsqrt(total * (1.0 / (width * blocks)) + EPS)
    row = lax.broadcasted_iota(jnp.int32, (8, mean.shape[1]), 0)
    column = rows_to_columns(jnp.where(row == 0, mean, jnp.where(row == 1, rstd, 0.0)))
    mean_ref[...] = jnp.broadcast_to(column[0], mean_ref.shape)
    rstd_ref[...] = jnp.broadcast_to(column[1], rstd_ref.shape)


def shift_rows(value, by):
    if by == 0:
        return value
    empty = jnp.zeros_like(value[:1])
    if by < 0:
        return jnp.concatenate([empty, value[:-1]], axis=0)
    return jnp.concatenate([value[1:], empty], axis=0)


def shift_columns(value, by):
    if by == 0:
        return value
    half = value.shape[1]
    place = lax.broadcasted_iota(jnp.int32, value.shape, 1)
    if by < 0:
        return jnp.where(place == 0, 0.0, pltpu.roll(value, 1, 1))
    return jnp.where(place == half - 1, 0.0, pltpu.roll(value, half - 1, 1))


def neighbours(grid_values):
    sides = {}
    for u in range(2):
        for v in range(2):
            for by in (0, -1 if v == 1 else 1):
                sides[u, v, by] = shift_columns(grid_values[u, v], by)
    found = {}
    for u in range(2):
        for v in range(2):
            for a in (-1, 0, 1):
                for b in (-1, 0, 1):
                    row, by_row = TAP[u, a]
                    column, by_column = TAP[v, b]
                    found[u, v, a, b] = shift_rows(sides[row, column, by_column], by_row)
    return found


def forward(pre, mean, rstd, gain, bias, taps, half):
    cells = half * half
    normed, shifted, sig, act, mixed = {}, {}, {}, {}, {}
    for u in range(2):
        for v in range(2):
            place = 2 * u + v
            rows = slice(place * cells, (place + 1) * cells)
            value = (pre[place] - mean[rows]) * rstd[rows]
            moved = value * gain + bias
            gate = sigmoid(moved)
            normed[u, v], shifted[u, v], sig[u, v] = value, moved, gate
            act[u, v] = (moved * gate).reshape(half, half, LANES)
    around = neighbours(act)
    for u in range(2):
        for v in range(2):
            total = None
            for a in (-1, 0, 1):
                for b in (-1, 0, 1):
                    part = taps[a + 1][b + 1] * around[u, v, a, b]
                    total = part if total is None else total + part
            mixed[u, v] = total
    return normed, shifted, sig, act, mixed, around


def load_taps(dw_ref):
    return [[dw_ref[3 * a + b : 3 * a + b + 1] for b in range(3)] for a in range(3)]


def maps_kernel(half, total_width, pre_ref, stat_ref, gain_ref, bias_ref, dw_ref, maps_ref, mean_ref, rstd_ref):
    cells = half * half

    @pl.when(pl.program_id(1) == 0)
    def _():
        spread_stats(stat_ref[0], total_width, mean_ref, rstd_ref)

    _, _, _, act, mixed, _ = forward(
        pre_ref[0], mean_ref[...], rstd_ref[...], gain_ref[...], bias_ref[...], load_taps(dw_ref), half
    )
    for u in range(2):
        for v in range(2):
            value = mixed[u, v]
            maps = act[u, v] + value * sigmoid(value)
            maps_ref[0, 2 * u + v] = maps.reshape(cells, LANES).astype(BF)


def maps_call(pre, stats, gain, bias, dw, half):
    count, phases, cells, width = pre.shape
    blocks = stats.shape[1]
    row = pl.BlockSpec((1, LANES), lambda p, c: (0, c))
    block = pl.BlockSpec((1, phases, cells, LANES), lambda p, c: (p, 0, 0, c))
    return pl.pallas_call(
        functools.partial(maps_kernel, half, width),
        grid=(count, width // LANES),
        in_specs=[
            block,
            pl.BlockSpec((1, blocks, 8, phases * cells), lambda p, c: (p, 0, 0, 0)),
            row,
            row,
            pl.BlockSpec((9, LANES), lambda p, c: (0, c)),
        ],
        out_specs=block,
        out_shape=jax.ShapeDtypeStruct(pre.shape, BF),
        scratch_shapes=[pltpu.VMEM((phases * cells, LANES), F32)] * 2,
        compiler_params=params(8),
        cost_estimate=pl.CostEstimate(
            flops=60 * pre.size,
            bytes_accessed=6 * pre.size,
            transcendentals=0,
        ),
        name="maps",
    )(pre, stats, gain, bias, dw)


def tube_kernel(count, source_ref, up_ref, *refs):
    maps_refs = refs[:count]
    w_ref, grad_ref, part_ref, held_ref, w_held, out_held, total_ref, near_ref, sorted_ref, sems = refs[count:]
    pairs, phases, cells, width = held_ref.shape

    copies, start = [], 0
    for place, ref in enumerate(maps_refs):
        copies.append(
            pltpu.make_async_copy(ref, held_ref.at[pl.ds(start, ref.shape[0])], sems.at[0, place])
        )
        start += ref.shape[0]
    loads = [pltpu.make_async_copy(w_ref.at[q], w_held.at[q], sems.at[1, q]) for q in range(phases)]
    stores = [
        pltpu.make_async_copy(out_held.at[q % 2], grad_ref.at[q], sems.at[2, q]) for q in range(phases)
    ]
    for copy in copies + loads:
        copy.start()
    for pair in range(pairs):
        near_ref[pair * cells : (pair + 1) * cells] = up_ref[source_ref[pair]]
    for copy in copies:
        copy.wait()
    for q in range(phases):
        rows = held_ref[:, q].reshape(pairs * cells, width)
        if q >= 2:
            stores[q - 2].wait()
        out_held[q % 2] = lax.dot_general(
            rows, near_ref[...], (((0,), (0,)), ((), ())), preferred_element_type=F32
        )
        stores[q].start()
        loads[q].wait()
        value = jnp.dot(rows, w_held[q], preferred_element_type=F32)
        if q == 0:
            total_ref[...] = value
        else:
            total_ref[...] += value
    for pair in range(pairs):
        sorted_ref[source_ref[pair]] = total_ref[pair * cells : (pair + 1) * cells]
    owners = part_ref.shape[0]
    held = cells // owners
    for owner in range(owners):
        part_ref[owner] = jnp.concatenate(
            [sorted_ref[pair, owner * held : (owner + 1) * held] for pair in range(pairs)], axis=0
        ).astype(BF)
    for copy in stores[-2:]:
        copy.wait()


def tube_call(source, maps, upstream, kernel, owners):
    phases, cells, width = maps[0].shape[1:]
    pairs, _, out_width = upstream.shape
    rows = pairs * cells
    return pl.pallas_call(
        functools.partial(tube_kernel, len(maps)),
        in_specs=[pl.BlockSpec(memory_space=pltpu.SMEM), pl.BlockSpec(memory_space=pltpu.VMEM)]
        + [pl.BlockSpec(memory_space=pl.ANY)] * (len(maps) + 1),
        out_specs=[
            pl.BlockSpec(memory_space=pl.ANY),
            pl.BlockSpec(memory_space=pltpu.VMEM),
        ],
        out_shape=[
            jax.ShapeDtypeStruct((phases, width, out_width), F32),
            jax.ShapeDtypeStruct((owners, rows // owners, out_width), BF),
        ],
        scratch_shapes=[
            pltpu.VMEM((pairs, phases, cells, width), BF),
            pltpu.VMEM((phases, width, out_width), BF),
            pltpu.VMEM((2, width, out_width), F32),
            pltpu.VMEM((rows, out_width), F32),
            pltpu.VMEM((rows, out_width), BF),
            pltpu.VMEM((pairs, cells, out_width), F32),
            pltpu.SemaphoreType.DMA((3, max(phases, len(maps)))),
        ],
        compiler_params=params(58),
        cost_estimate=pl.CostEstimate(
            flops=4 * rows * phases * width * out_width,
            bytes_accessed=6 * phases * width * out_width,
            transcendentals=0,
        ),
        name="tube",
    )(source, upstream, *maps, kernel)


def back_kernel(half, total_width, count, pre_ref, stat_ref, gain_ref, bias_ref, dw_ref, *refs):
    grad_refs = refs[:count]
    scaled_ref, sums_ref, back_ref, mean_ref, rstd_ref, first_ref, second_ref = refs[count:]
    step, steps = pl.program_id(0), pl.num_programs(0)
    cells = half * half

    @pl.when(step == 0)
    def _():
        spread_stats(stat_ref[0], total_width, mean_ref, rstd_ref)
        first_ref[...] = jnp.zeros_like(first_ref)
        second_ref[...] = jnp.zeros_like(second_ref)

    taps = load_taps(dw_ref)
    gain = gain_ref[...]
    normed, shifted, sig, _, mixed, around = forward(
        pre_ref[0], mean_ref[...], rstd_ref[...], gain, bias_ref[...], taps, half
    )
    grad_maps, grad_mixed = {}, {}
    for u in range(2):
        for v in range(2):
            value = mixed[u, v]
            gate = sigmoid(value)
            slope = gate * (1.0 + value * (1.0 - gate))
            grad = grad_refs[0][0, 2 * u + v].astype(F32)
            for ref in grad_refs[1:]:
                grad = grad + ref[0, 2 * u + v].astype(F32)
            grad = grad.reshape(half, half, LANES)
            grad_maps[u, v] = grad
            grad_mixed[u, v] = grad * slope
    for a in (-1, 0, 1):
        for b in (-1, 0, 1):
            total = None
            for u in range(2):
                for v in range(2):
                    part = grad_mixed[u, v] * around[u, v, a, b]
                    total = part if total is None else total + part
            place = 3 * (a + 1) + b + 1
            sums_ref[place : place + 1] = jnp.sum(
                total.reshape(cells, LANES), axis=0, keepdims=True
            )
    spread = neighbours(grad_mixed)
    gain_total, bias_total = None, None
    for u in range(2):
        for v in range(2):
            total = grad_maps[u, v]
            for a in (-1, 0, 1):
                for b in (-1, 0, 1):
                    total = total + taps[a + 1][b + 1] * spread[u, v, -a, -b]
            gate, value = sig[u, v], shifted[u, v]
            grad_shift = total.reshape(cells, LANES) * (gate * (1.0 + value * (1.0 - gate)))
            along = grad_shift * normed[u, v]
            gain_total = along if gain_total is None else gain_total + along
            bias_total = grad_shift if bias_total is None else bias_total + grad_shift
            scaled = grad_shift * gain
            rows = slice((2 * u + v) * cells, (2 * u + v + 1) * cells)
            scaled_ref[rows] = scaled
            first_ref[rows] += scaled
            second_ref[rows] += along * gain
    sums_ref[9:10] = jnp.sum(gain_total, axis=0, keepdims=True)
    sums_ref[10:11] = jnp.sum(bias_total, axis=0, keepdims=True)
    sums_ref[11:16] = jnp.zeros((5, LANES), F32)

    @pl.when(step == steps - 1)
    def _():
        back_ref[...] = columns_to_rows(
            [
                jnp.sum(first_ref[...], axis=1, keepdims=True),
                jnp.sum(second_ref[...], axis=1, keepdims=True),
            ]
        )


def back_call(pre, stats, grad_maps, gain, bias, dw, half):
    _, phases, cells, width = pre.shape
    blocks = stats.shape[1]
    tokens = phases * cells
    row = pl.BlockSpec((1, LANES), lambda c: (0, c))
    block = pl.BlockSpec((1, phases, cells, LANES), lambda c: (0, 0, 0, c))
    return pl.pallas_call(
        functools.partial(back_kernel, half, width, len(grad_maps)),
        grid=(width // LANES,),
        in_specs=[
            block,
            pl.BlockSpec((1, blocks, 8, tokens), lambda c: (0, 0, 0, 0)),
            row,
            row,
            pl.BlockSpec((9, LANES), lambda c: (0, c)),
        ]
        + [block] * len(grad_maps),
        out_specs=[
            pl.BlockSpec((tokens, LANES), lambda c: (0, c)),
            pl.BlockSpec((16, LANES), lambda c: (0, c)),
            pl.BlockSpec((8, tokens), lambda c: (0, 0)),
        ],
        out_shape=[
            jax.ShapeDtypeStruct((tokens, width), F32),
            jax.ShapeDtypeStruct((16, width), F32),
            jax.ShapeDtypeStruct((8, tokens), F32),
        ],
        scratch_shapes=[pltpu.VMEM((tokens, LANES), F32)] * 4,
        compiler_params=params(8),
        cost_estimate=pl.CostEstimate(
            flops=150 * pre.size,
            bytes_accessed=10 * pre.size,
            transcendentals=0,
        ),
        name="back",
    )(pre, stats, gain, bias, dw, *grad_maps)


def turn_kernel(
    total_width, scaled_ref, pre_ref, stat_ref, back_ref, sums_ref, out_ref, mean_ref, rstd_ref, first_ref, second_ref
):
    tokens, width = scaled_ref.shape
    owners, rows, _ = out_ref.shape
    share = width // owners
    spread_stats(stat_ref[0], total_width, mean_ref, rstd_ref)
    column = rows_to_columns(
        jnp.sum(back_ref[...], axis=0) * (1.0 / (total_width * back_ref.shape[0]))
    )
    first_ref[...] = jnp.broadcast_to(column[0], first_ref.shape)
    second_ref[...] = jnp.broadcast_to(column[1], second_ref.shape)
    mean, rstd, first, second = mean_ref[...], rstd_ref[...], first_ref[...], second_ref[...]
    for part in range(width // LANES):
        lanes = slice(part * LANES, (part + 1) * LANES)
        normed = (pre_ref[0, :, :, lanes].reshape(tokens, LANES) - mean) * rstd
        grad = ((scaled_ref[:, lanes] - first - normed * second) * rstd).T.astype(BF)
        row = part * LANES
        while row < (part + 1) * LANES:
            owner, place = divmod(row, share)
            count = min(share - place, (part + 1) * LANES - row)
            out_ref[owner, place : place + count] = grad[row - part * LANES : row - part * LANES + count]
            row += count
    for owner in range(owners):
        if rows - 16 > share:
            out_ref[owner, share : rows - 16] = jnp.zeros((rows - 16 - share, tokens), BF)
        value = sums_ref[:, owner * share : (owner + 1) * share]
        large = value.astype(BF)
        small = (value - large.astype(F32)).astype(BF)
        edge = jnp.zeros((16, LANES - share), BF)
        out_ref[owner, rows - 16 :, :LANES] = jnp.concatenate([large, edge], axis=1)
        out_ref[owner, rows - 16 :, LANES:] = jnp.concatenate([small, edge], axis=1)


def turn_call(scaled, pre, stats, back, sums, owners):
    tokens, width = scaled.shape
    rows = -(-(width // owners) // 16) * 16 + 16
    return pl.pallas_call(
        functools.partial(turn_kernel, width),
        out_shape=jax.ShapeDtypeStruct((owners, rows, tokens), BF),
        scratch_shapes=[pltpu.VMEM((tokens, LANES), F32)] * 4,
        compiler_params=params(10),
        cost_estimate=pl.CostEstimate(
            flops=8 * scaled.size,
            bytes_accessed=10 * scaled.size,
            transcendentals=0,
        ),
        name="turn",
    )(scaled, pre, stats, back, sums)


def weight_kernel(counts, info_ref, grad_ref, *refs):
    total_pieces = sum(counts)
    pieces = refs[:total_pieces]
    out_ref, dw_ref, gain_ref, bias_ref, rows_ref, held_ref, total_ref, sems = refs[total_pieces:]
    groups, frame = len(counts), grad_ref.shape[2]
    cells = frame // 4
    share = out_ref.shape[0]
    slots = held_ref.shape[0]

    def copies(group):
        first = sum(counts[:group])
        length = frame // counts[group]
        return [
            pltpu.make_async_copy(
                pieces[first + i],
                held_ref.at[group % slots, pl.ds(i * length, length)],
                sems.at[group % slots, i],
            )
            for i in range(counts[group])
        ]

    for group in range(min(slots, groups)):
        for copy in copies(group):
            copy.start()

    own = info_ref[0]
    if share < LANES:
        rows_ref[:, share:] = jnp.zeros((groups, LANES - share, frame), BF)
    for group in range(groups):
        value = grad_ref[info_ref[1 + group], :share].astype(F32)
        if group:
            value = jnp.where((own & 2) == 2, pltpu.roll(value, 2 * cells, 1), value)
            part = lax.broadcasted_iota(jnp.int32, value.shape, 1) // cells
            swapped = jnp.where(
                (part & 1) == 0, pltpu.roll(value, 3 * cells, 1), pltpu.roll(value, cells, 1)
            )
            value = jnp.where((own & 1) == 1, swapped, value)
        rows_ref[group, :share] = value.astype(BF)
    total = jnp.zeros((16, LANES), F32)
    for group in range(groups):
        tail = grad_ref[group, grad_ref.shape[1] - 16 :].astype(F32)
        total = total + tail[:, :LANES] + tail[:, LANES : 2 * LANES]
    for row in range(3):
        dw_ref[row] = total[3 * row : 3 * row + 3, :share]
    gain_ref[...] = total[9:10, :share]
    bias_ref[...] = total[10:11, :share]

    for group in range(groups):
        for copy in copies(group):
            copy.wait()
        value = jnp.dot(rows_ref[group], held_ref[group % slots], preferred_element_type=F32)
        if group == 0:
            total_ref[...] = value
        elif group < groups - 1:
            total_ref[...] += value
        else:
            out_ref[...] = (total_ref[...] + value)[:share]
        if group + slots < groups:
            for copy in copies(group + slots):
                copy.start()


def weight_call(info, groups, grad, share):
    count, rows, tokens = grad.shape
    depth = groups[0][0].shape[1]
    pieces = [piece for group in groups for piece in group]
    slots = min(count, 8)
    return pl.pallas_call(
        functools.partial(weight_kernel, [len(group) for group in groups]),
        in_specs=[
            pl.BlockSpec(memory_space=pltpu.SMEM),
            pl.BlockSpec(memory_space=pltpu.VMEM),
        ]
        + [pl.BlockSpec(memory_space=pl.ANY)] * len(pieces),
        out_specs=[pl.BlockSpec(memory_space=pltpu.VMEM)] * 4,
        out_shape=[
            jax.ShapeDtypeStruct((share, depth), F32),
            jax.ShapeDtypeStruct((3, 3, share), F32),
            jax.ShapeDtypeStruct((1, share), F32),
            jax.ShapeDtypeStruct((1, share), F32),
        ],
        scratch_shapes=[
            pltpu.VMEM((count, LANES, tokens), BF),
            pltpu.VMEM((slots, tokens, depth), BF),
            pltpu.VMEM((LANES, depth), F32),
            pltpu.SemaphoreType.DMA((slots, 4)),
        ],
        compiler_params=params(60),
        cost_estimate=pl.CostEstimate(
            flops=2 * LANES * count * tokens * depth,
            bytes_accessed=2 * count * tokens * depth,
            transcendentals=0,
        ),
        name="weight",
    )(info, grad, *pieces)


def tie(value, *before):
    return lax.optimization_barrier((value, before))[0]


def together(*values):
    return lax.optimization_barrier(values)


def shards(patches, w_in, ln_gain, ln_bias, dw_kernel, w_tube, grad_out, clip_frames, clip_batch):
    ranks, sections, blocks = lax.axis_size("dp"), lax.axis_size("section"), lax.axis_size("mp")
    rank, side, own = lax.axis_index("dp"), lax.axis_index("section"), lax.axis_index("mp")
    grid, depth = patches.shape[2], patches.shape[4]
    half = grid // 2
    cells = half * half
    width = w_in.shape[1]
    out_width = w_tube.shape[4]
    total_pairs = grad_out.shape[0]
    share = width // (ranks * sections)
    gain, bias = ln_gain[None, :], ln_bias[None, :]
    dw = dw_kernel.reshape(9, width)
    kernel = w_tube.reshape(4, width, out_width)
    straight = jnp.arange(4, dtype=jnp.int32)
    order = own ^ straight
    swap = [(i, (i + 1) % sections) for i in range(sections)]
    source = (rank ^ jnp.arange(ranks, dtype=jnp.int32)).astype(jnp.int32)

    def over_x(value):
        return lax.ppermute(value, "mp", CROSS)

    def over_core(value):
        return lax.ppermute(value, "mp", CORE)

    def over_y(value):
        return lax.ppermute(value, "section", swap)

    def norm_stats(stat):
        return lax.all_gather(stat, "mp", axis=1)

    def over_z(value, mask):
        return lax.ppermute(value, "dp", [(i, i ^ mask) for i in range(ranks)])

    rows = patches.reshape(grid * grid, depth)
    piece = phase_call(own[None].astype(jnp.int32), rows, 1, half)
    early = over_z(piece, 1)
    other = phase_call(own[None].astype(jnp.int32) ^ 2, tie(rows, piece), 1, half)
    across, across_x = [over_y(piece)], [over_y(other)]

    weight = pair_scale(clip_frames, clip_batch, total_pairs, clip_frames.shape[0])
    upstream = (tie(grad_out, piece).astype(F32) * weight[:, None, None]).astype(BF)
    later = tie(piece, upstream)
    fetched = [over_z(later, mask) for mask in range(2, ranks)]
    even, odd = term_call(rank[None].astype(jnp.int32), upstream, kernel)
    phased = phase_call(straight[:1], tie(rows, even), 4, half)
    own_pre, own_stat = pre_call(straight, [[phased]], w_in, cells)
    own_stat = norm_stats(own_stat)
    own_stat, early, across, across_x, odd = together(own_stat, early, across, across_x, odd)
    taken = over_z(odd, 1)
    crossed = [over_x(early)]
    across.append(over_y(early))
    own_maps = maps_call(own_pre, own_stat, gain, bias, dw, half)
    own_maps, early, fetched, crossed, across = together(
        own_maps, early, fetched, crossed, across
    )

    crossed += [over_x(value) for value in fetched]
    groups = [[early, over_core(early), crossed[0], over_core(crossed[0])]]
    pre, stat = pre_call(order, groups, w_in, cells)
    pre, stat, taken = together(pre, stat, taken)
    pres, stats = [pre], [stat]
    grad_maps, rest, step = [even], even[1:], 2
    while step < ranks:
        grad_maps.append(taken)
        rest = (rest.astype(F32) + taken[1:].astype(F32)).astype(BF)
        taken = over_z(rest[::2], step)
        rest = rest[1::2]
        step *= 2
    grad_maps.append(taken)
    across += [over_y(value) for value in fetched]
    across_x.append(over_y(crossed[0]))
    pres, stats, crossed[1:], fetched, across = together(
        pres, stats, crossed[1:], fetched, across
    )
    groups += [[a, over_core(a), b, over_core(b)] for a, b in zip(fetched, crossed[1:])]
    for start in range(1, ranks - 1, 2):
        pre, stat = pre_call(order, groups[start : start + 2], w_in, cells)
        pres.append(pre)
        stats.append(stat)
    pres, stats, grad_maps = together(pres, stats, grad_maps)
    across_x += [over_y(tie(value, stats)) for value in crossed[1:-1]]
    across_x.append(over_x(tie(across[-1], stats)))

    scaled, sums, back = back_call(own_pre, own_stat, grad_maps, gain, bias, dw, half)
    stat = norm_stats(tie(jnp.concatenate(stats + [back[None]], axis=0), across_x[-1]))
    stat, back = stat[:-1], stat[-1]
    turned = turn_call(scaled, own_pre, own_stat, back, sums, ranks * sections)
    turned, stat, across, across_x = together(turned, stat, across, across_x)
    received = lax.all_to_all(turned, ("dp", "section"), 0, 0, tiled=True)
    across = [[a, over_core(a), b, over_core(b)] for a, b in zip(across, across_x)]
    maps, start = [own_maps], 0
    for pre in pres:
        part = stat[start : start + pre.shape[0]]
        maps.append(maps_call(pre, part, gain, bias, dw, half))
        start += pre.shape[0]
    grad_w_tube, partial = tube_call(source, maps, upstream, kernel, sections * blocks)
    partial, received, across = together(partial, received, across)
    partial = lax.all_to_all(partial, ("section", "mp"), 0, 0, tiled=True)
    place = jnp.concatenate([source * sections + side, source * sections + (sections - 1 - side)])
    info = jnp.concatenate([own[None], place]).astype(jnp.int32)
    grad_w_in, grad_dw, grad_gain, grad_bias = weight_call(
        info, [[phased]] + groups + across, received, share
    )
    partial, grad_w_in = together(partial, grad_w_in)
    tubes = jnp.sum(partial.astype(F32), axis=0).astype(BF).reshape(total_pairs, -1, out_width)
    return (
        tubes,
        grad_w_in.T,
        grad_gain.reshape(share),
        grad_bias.reshape(share),
        grad_dw,
        grad_w_tube.reshape(w_tube.shape),
    )


def solution(mesh):
    placed = (
        P("dp", "section", None, None, None),
        P(None, "mp"),
        P("mp"),
        P("mp"),
        P(None, None, "mp"),
        P("section", None, None, "mp", "dp"),
        P(None, None, "dp"),
        P(),
        P(),
    )
    return jax.shard_map(
        shards,
        mesh=mesh,
        in_specs=placed,
        out_specs=(
            P(None, ("section", "mp"), "dp"),
            P(None, ("mp", "dp", "section")),
            P(("mp", "dp", "section")),
            P(("mp", "dp", "section")),
            P(None, None, ("mp", "dp", "section")),
            P("section", None, None, "mp", "dp"),
        ),
        check_vma=False,
    )
```

```python
import functools

import jax
import jax.numpy as jnp
from jax import lax
from jax.experimental import pallas as pl
from jax.experimental.pallas import tpu as pltpu
from jax.sharding import PartitionSpec as P

CH = 3584
MICRO = 4
EPS = 1e-06
SMALL = pl.CostEstimate(flops=1, bytes_accessed=1, transcendentals=0)
LANES = 128
BF = jnp.bfloat16
F32 = jnp.float32
CORE = [(0, 1), (1, 0), (2, 3), (3, 2)]
CROSS = [(0, 2), (2, 0), (1, 3), (3, 1)]
TAP = {(u, a): ((u + a) % 2, (u + a) // 2) for u in range(2) for a in (-1, 0, 1)}


def params(mib):
    return pltpu.CompilerParams(vmem_limit_bytes=mib * 2**20)


def pair_scale(clip_frames, clip_batch, count, nclip):
    halves = clip_frames // 2
    ends = jnp.cumsum(halves)
    starts = ends - halves
    places = jnp.arange(count, dtype=jnp.int32)
    member = ((places[:, None] >= starts[None, :]) & (places[:, None] < ends[None, :])).astype(F32)
    batch_hot = (clip_batch[:, None] == jnp.arange(MICRO, dtype=jnp.int32)[None, :]).astype(F32)
    batch_pairs = jnp.sum(batch_hot * halves.astype(F32)[:, None], axis=0)
    clip_load = jnp.sum(batch_hot * batch_pairs[None, :], axis=1)
    clip_scale = 10.0 * nclip / (MICRO * clip_load)
    return jnp.sum(member * clip_scale[None, :], axis=1)


def sigmoid(value):
    return 0.5 + 0.5 * jnp.tanh(0.5 * value)


def columns_to_rows(columns):
    rows = columns[0].shape[0]
    lane = lax.broadcasted_iota(jnp.int32, (rows, LANES), 1)
    wide = jnp.zeros((rows, LANES), F32)
    for place, column in enumerate(columns):
        wide = jnp.where(lane == place, column, wide)
    return wide.T[:8]


def rows_to_columns(stacked):
    padded = jnp.concatenate([stacked, jnp.zeros((LANES - 8, stacked.shape[1]), F32)], axis=0)
    turned = padded.T
    return [turned[:, place : place + 1] for place in range(8)]


def term_kernel(rank_ref, up_ref, w_ref, even_ref, odd_ref, rows_ref):
    half_ranks, _, cells, width = even_ref.shape
    ranks = 2 * half_ranks

    @pl.when(pl.program_id(0) == 0)
    def _():
        for place in range(ranks):
            rows_ref[place * cells : (place + 1) * cells] = up_ref[rank_ref[0] ^ place]

    value = lax.dot_general(
        rows_ref[...], w_ref[0], (((1,), (1,)), ((), ())), preferred_element_type=F32
    ).astype(BF)
    for place in range(ranks):
        out_ref = odd_ref if place % 2 else even_ref
        out_ref[place // 2, 0] = value[place * cells : (place + 1) * cells]


def term_call(rank, upstream, kernel):
    pairs, cells, out_width = upstream.shape
    phases, width, _ = kernel.shape
    block = pl.BlockSpec((pairs // 2, 1, cells, width), lambda q, rank: (0, q, 0, 0))
    return pl.pallas_call(
        term_kernel,
        grid_spec=pltpu.PrefetchScalarGridSpec(
            num_scalar_prefetch=1,
            grid=(phases,),
            in_specs=[
                pl.BlockSpec((pairs, cells, out_width), lambda q, rank: (0, 0, 0)),
                pl.BlockSpec((1, width, out_width), lambda q, rank: (q, 0, 0)),
            ],
            out_specs=[block, block],
            scratch_shapes=[pltpu.VMEM((pairs * cells, out_width), BF)],
        ),
        out_shape=[jax.ShapeDtypeStruct((pairs // 2, phases, cells, width), BF)] * 2,
        compiler_params=params(24),
        cost_estimate=pl.CostEstimate(
            flops=2 * pairs * cells * phases * width * out_width,
            bytes_accessed=2 * phases * width * (out_width + pairs * cells),
            transcendentals=0,
        ),
        name="term",
    )(rank, upstream, kernel)


def phase_rows(shape, first, half):
    row = lax.broadcasted_iota(jnp.int32, shape, 0) + first * half * half
    token = lax.broadcasted_iota(jnp.int32, shape, 1)
    phase, cell = row // (half * half), row % (half * half)
    wanted = 2 * half * (2 * (cell // half) + phase // 2) + 2 * (cell % half) + phase % 2
    return jnp.where(token == wanted, 1.0, 0.0).astype(BF)


def phase_kernel(half, first_ref, rows_ref, out_ref):
    hot = phase_rows((out_ref.shape[0], rows_ref.shape[0]), first_ref[0], half)
    out_ref[...] = jnp.dot(hot, rows_ref[...], preferred_element_type=F32).astype(BF)


def phase_call(first, rows, count, half):
    tokens, depth = rows.shape
    out_rows = count * half * half
    return pl.pallas_call(
        functools.partial(phase_kernel, half),
        grid_spec=pltpu.PrefetchScalarGridSpec(
            num_scalar_prefetch=1,
            grid=(1,),
            in_specs=[pl.BlockSpec((tokens, depth), lambda k, first: (0, 0))],
            out_specs=pl.BlockSpec((out_rows, depth), lambda k, first: (0, 0)),
        ),
        out_shape=jax.ShapeDtypeStruct((out_rows, depth), BF),
        compiler_params=params(12),
        cost_estimate=pl.CostEstimate(
            flops=2 * tokens * out_rows * depth,
            bytes_accessed=2 * depth * (tokens + out_rows),
            transcendentals=0,
        ),
        name="phase",
    )(first, rows)


def pre_kernel(groups, cuts, order_ref, *refs):
    pieces, (w_ref, pre_ref, stat_ref, held_ref, total_ref, sems) = refs[:-6], refs[-6:]
    width = w_ref.shape[1]
    cells = pre_ref.shape[2]
    frame = 4 * cells
    parts = [slice(low, high) for low, high in zip(cuts[:-1], cuts[1:])]
    copies = [
        pltpu.make_async_copy(w_ref.at[part], held_ref.at[part], sems.at[place])
        for place, part in enumerate(parts)
    ]
    for copy in copies:
        copy.start()
    for place, part in enumerate(parts):
        copies[place].wait()
        rows = jnp.concatenate([ref[:, part] for ref in pieces], axis=0)
        value = jnp.dot(rows, held_ref[part], preferred_element_type=F32)
        if place == 0:
            total_ref[...] = value
        elif place < len(parts) - 1:
            total_ref[...] += value
    value = total_ref[...] + value
    for group in range(groups):
        for place in range(4):
            start = group * frame + place * cells
            pre_ref[group, order_ref[place]] = value[start : start + cells]
        part = pre_ref[group].reshape(frame, width)
        mean = jnp.sum(part, axis=1, keepdims=True) * (1.0 / width)
        apart = part - mean
        spread = jnp.sum(apart * apart, axis=1, keepdims=True)
        stat_ref[group] = columns_to_rows([mean, spread])


def pre_call(order, groups, w_in, cells):
    depth, width = w_in.shape
    count = len(groups)
    pieces = [piece for group in groups for piece in group]
    quarter = -(-depth // 1024) * 256
    cuts = list(range(0, depth - quarter // 2, quarter)) + [depth]
    return pl.pallas_call(
        functools.partial(pre_kernel, count, cuts),
        grid_spec=pltpu.PrefetchScalarGridSpec(
            num_scalar_prefetch=1,
            grid=(),
            in_specs=[pl.BlockSpec(memory_space=pltpu.VMEM)] * len(pieces)
            + [pl.BlockSpec(memory_space=pltpu.HBM)],
            out_specs=[pl.BlockSpec(memory_space=pltpu.VMEM)] * 2,
            scratch_shapes=[
                pltpu.VMEM((depth, width), BF),
                pltpu.VMEM((4 * count * cells, width), F32),
                pltpu.SemaphoreType.DMA((len(cuts) - 1,)),
            ],
        ),
        out_shape=[
            jax.ShapeDtypeStruct((count, 4, cells, width), F32),
            jax.ShapeDtypeStruct((count, 8, 4 * cells), F32),
        ],
        compiler_params=params(24),
        cost_estimate=SMALL,
        name="pre",
    )(order, *pieces, w_in)


def spread_stats(stats, width, mean_ref, rstd_ref):
    blocks = stats.shape[0]
    means, spreads = stats[:, 0], stats[:, 1]
    mean = jnp.sum(means, axis=0, keepdims=True) * (1.0 / blocks)
    apart = means - mean
    total = jnp.sum(spreads, axis=0, keepdims=True) + width * jnp.sum(
        apart * apart, axis=0, keepdims=True
    )
    rstd = lax.rsqrt(total * (1.0 / (width * blocks)) + EPS)
    row = lax.broadcasted_iota(jnp.int32, (8, mean.shape[1]), 0)
    column = rows_to_columns(jnp.where(row == 0, mean, jnp.where(row == 1, rstd, 0.0)))
    mean_ref[...] = jnp.broadcast_to(column[0], mean_ref.shape)
    rstd_ref[...] = jnp.broadcast_to(column[1], rstd_ref.shape)


def shift_rows(value, by):
    if by == 0:
        return value
    empty = jnp.zeros_like(value[:1])
    if by < 0:
        return jnp.concatenate([empty, value[:-1]], axis=0)
    return jnp.concatenate([value[1:], empty], axis=0)


def shift_columns(value, by):
    if by == 0:
        return value
    half = value.shape[1]
    place = lax.broadcasted_iota(jnp.int32, value.shape, 1)
    if by < 0:
        return jnp.where(place == 0, 0.0, pltpu.roll(value, 1, 1))
    return jnp.where(place == half - 1, 0.0, pltpu.roll(value, half - 1, 1))


def neighbours(grid_values):
    sides = {}
    for u in range(2):
        for v in range(2):
            for by in (0, -1 if v == 1 else 1):
                sides[u, v, by] = shift_columns(grid_values[u, v], by)
    found = {}
    for u in range(2):
        for v in range(2):
            for a in (-1, 0, 1):
                for b in (-1, 0, 1):
                    row, by_row = TAP[u, a]
                    column, by_column = TAP[v, b]
                    found[u, v, a, b] = shift_rows(sides[row, column, by_column], by_row)
    return found


def forward(pre, mean, rstd, gain, bias, taps, half):
    cells = half * half
    normed, shifted, sig, act, mixed = {}, {}, {}, {}, {}
    for u in range(2):
        for v in range(2):
            place = 2 * u + v
            rows = slice(place * cells, (place + 1) * cells)
            value = (pre[place] - mean[rows]) * rstd[rows]
            moved = value * gain + bias
            gate = sigmoid(moved)
            normed[u, v], shifted[u, v], sig[u, v] = value, moved, gate
            act[u, v] = (moved * gate).reshape(half, half, LANES)
    around = neighbours(act)
    for u in range(2):
        for v in range(2):
            total = None
            for a in (-1, 0, 1):
                for b in (-1, 0, 1):
                    part = taps[a + 1][b + 1] * around[u, v, a, b]
                    total = part if total is None else total + part
            mixed[u, v] = total
    return normed, shifted, sig, act, mixed, around


def load_taps(dw_ref):
    return [[dw_ref[3 * a + b : 3 * a + b + 1] for b in range(3)] for a in range(3)]


def maps_kernel(half, total_width, pre_ref, stat_ref, gain_ref, bias_ref, dw_ref, maps_ref, mean_ref, rstd_ref):
    cells = half * half

    @pl.when(pl.program_id(1) == 0)
    def _():
        spread_stats(stat_ref[0], total_width, mean_ref, rstd_ref)

    _, _, _, act, mixed, _ = forward(
        pre_ref[0], mean_ref[...], rstd_ref[...], gain_ref[...], bias_ref[...], load_taps(dw_ref), half
    )
    for u in range(2):
        for v in range(2):
            value = mixed[u, v]
            maps = act[u, v] + value * sigmoid(value)
            maps_ref[0, 2 * u + v] = maps.reshape(cells, LANES).astype(BF)


def maps_call(pre, stats, gain, bias, dw, half):
    count, phases, cells, width = pre.shape
    blocks = stats.shape[1]
    row = pl.BlockSpec((1, LANES), lambda p, c: (0, c))
    block = pl.BlockSpec((1, phases, cells, LANES), lambda p, c: (p, 0, 0, c))
    return pl.pallas_call(
        functools.partial(maps_kernel, half, width),
        grid=(count, width // LANES),
        in_specs=[
            block,
            pl.BlockSpec((1, blocks, 8, phases * cells), lambda p, c: (p, 0, 0, 0)),
            row,
            row,
            pl.BlockSpec((9, LANES), lambda p, c: (0, c)),
        ],
        out_specs=block,
        out_shape=jax.ShapeDtypeStruct(pre.shape, BF),
        scratch_shapes=[pltpu.VMEM((phases * cells, LANES), F32)] * 2,
        compiler_params=params(8),
        cost_estimate=pl.CostEstimate(
            flops=60 * pre.size,
            bytes_accessed=6 * pre.size,
            transcendentals=0,
        ),
        name="maps",
    )(pre, stats, gain, bias, dw)


def tube_kernel(count, source_ref, up_ref, *refs):
    maps_refs = refs[:count]
    w_ref, grad_ref, part_ref, held_ref, w_held, out_held, total_ref, near_ref, sorted_ref, sems = refs[count:]
    pairs, phases, cells, width = held_ref.shape

    copies, start = [], 0
    for place, ref in enumerate(maps_refs):
        copies.append(
            pltpu.make_async_copy(ref, held_ref.at[pl.ds(start, ref.shape[0])], sems.at[0, place])
        )
        start += ref.shape[0]
    loads = [pltpu.make_async_copy(w_ref.at[q], w_held.at[q], sems.at[1, q]) for q in range(phases)]
    stores = [
        pltpu.make_async_copy(out_held.at[q % 2], grad_ref.at[q], sems.at[2, q]) for q in range(phases)
    ]
    for copy in copies:
        copy.start()
    for pair in range(pairs):
        near_ref[pair * cells : (pair + 1) * cells] = up_ref[source_ref[pair]]
    for copy in copies:
        copy.wait()
    for copy in loads:
        copy.start()
    for q in range(phases):
        rows = held_ref[:, q].reshape(pairs * cells, width)
        if q >= 2:
            stores[q - 2].wait()
        out_held[q % 2] = lax.dot_general(
            rows, near_ref[...], (((0,), (0,)), ((), ())), preferred_element_type=F32
        )
        stores[q].start()
        loads[q].wait()
        value = jnp.dot(rows, w_held[q], preferred_element_type=F32)
        if q == 0:
            total_ref[...] = value
        else:
            total_ref[...] += value
    for pair in range(pairs):
        sorted_ref[source_ref[pair]] = total_ref[pair * cells : (pair + 1) * cells]
    owners = part_ref.shape[0]
    held = cells // owners
    for owner in range(owners):
        part_ref[owner] = jnp.concatenate(
            [sorted_ref[pair, owner * held : (owner + 1) * held] for pair in range(pairs)], axis=0
        ).astype(BF)
    for copy in stores[-2:]:
        copy.wait()


def tube_call(source, maps, upstream, kernel, owners):
    phases, cells, width = maps[0].shape[1:]
    pairs, _, out_width = upstream.shape
    rows = pairs * cells
    return pl.pallas_call(
        functools.partial(tube_kernel, len(maps)),
        in_specs=[pl.BlockSpec(memory_space=pltpu.SMEM), pl.BlockSpec(memory_space=pltpu.VMEM)]
        + [pl.BlockSpec(memory_space=pl.ANY)] * (len(maps) + 1),
        out_specs=[
            pl.BlockSpec(memory_space=pl.ANY),
            pl.BlockSpec(memory_space=pltpu.VMEM),
        ],
        out_shape=[
            jax.ShapeDtypeStruct((phases, width, out_width), F32),
            jax.ShapeDtypeStruct((owners, rows // owners, out_width), BF),
        ],
        scratch_shapes=[
            pltpu.VMEM((pairs, phases, cells, width), BF),
            pltpu.VMEM((phases, width, out_width), BF),
            pltpu.VMEM((2, width, out_width), F32),
            pltpu.VMEM((rows, out_width), F32),
            pltpu.VMEM((rows, out_width), BF),
            pltpu.VMEM((pairs, cells, out_width), F32),
            pltpu.SemaphoreType.DMA((3, max(phases, len(maps)))),
        ],
        compiler_params=params(58),
        cost_estimate=pl.CostEstimate(
            flops=4 * rows * phases * width * out_width,
            bytes_accessed=6 * phases * width * out_width,
            transcendentals=0,
        ),
        name="tube",
    )(source, upstream, *maps, kernel)


def back_kernel(half, total_width, count, pre_ref, stat_ref, gain_ref, bias_ref, dw_ref, *refs):
    grad_refs = refs[:count]
    scaled_ref, sums_ref, back_ref, mean_ref, rstd_ref, first_ref, second_ref = refs[count:]
    step, steps = pl.program_id(0), pl.num_programs(0)
    cells = half * half

    @pl.when(step == 0)
    def _():
        spread_stats(stat_ref[0], total_width, mean_ref, rstd_ref)
        first_ref[...] = jnp.zeros_like(first_ref)
        second_ref[...] = jnp.zeros_like(second_ref)

    taps = load_taps(dw_ref)
    gain = gain_ref[...]
    normed, shifted, sig, _, mixed, around = forward(
        pre_ref[0], mean_ref[...], rstd_ref[...], gain, bias_ref[...], taps, half
    )
    grad_maps, grad_mixed = {}, {}
    for u in range(2):
        for v in range(2):
            value = mixed[u, v]
            gate = sigmoid(value)
            slope = gate * (1.0 + value * (1.0 - gate))
            grad = grad_refs[0][0, 2 * u + v].astype(F32)
            for ref in grad_refs[1:]:
                grad = grad + ref[0, 2 * u + v].astype(F32)
            grad = grad.reshape(half, half, LANES)
            grad_maps[u, v] = grad
            grad_mixed[u, v] = grad * slope
    for a in (-1, 0, 1):
        for b in (-1, 0, 1):
            total = None
            for u in range(2):
                for v in range(2):
                    part = grad_mixed[u, v] * around[u, v, a, b]
                    total = part if total is None else total + part
            place = 3 * (a + 1) + b + 1
            sums_ref[place : place + 1] = jnp.sum(
                total.reshape(cells, LANES), axis=0, keepdims=True
            )
    spread = neighbours(grad_mixed)
    gain_total, bias_total = None, None
    for u in range(2):
        for v in range(2):
            total = grad_maps[u, v]
            for a in (-1, 0, 1):
                for b in (-1, 0, 1):
                    total = total + taps[a + 1][b + 1] * spread[u, v, -a, -b]
            gate, value = sig[u, v], shifted[u, v]
            grad_shift = total.reshape(cells, LANES) * (gate * (1.0 + value * (1.0 - gate)))
            along = grad_shift * normed[u, v]
            gain_total = along if gain_total is None else gain_total + along
            bias_total = grad_shift if bias_total is None else bias_total + grad_shift
            scaled = grad_shift * gain
            rows = slice((2 * u + v) * cells, (2 * u + v + 1) * cells)
            scaled_ref[rows] = scaled
            first_ref[rows] += scaled
            second_ref[rows] += along * gain
    sums_ref[9:10] = jnp.sum(gain_total, axis=0, keepdims=True)
    sums_ref[10:11] = jnp.sum(bias_total, axis=0, keepdims=True)
    sums_ref[11:16] = jnp.zeros((5, LANES), F32)

    @pl.when(step == steps - 1)
    def _():
        back_ref[...] = columns_to_rows(
            [
                jnp.sum(first_ref[...], axis=1, keepdims=True),
                jnp.sum(second_ref[...], axis=1, keepdims=True),
            ]
        )


def back_call(pre, stats, grad_maps, gain, bias, dw, half):
    _, phases, cells, width = pre.shape
    blocks = stats.shape[1]
    tokens = phases * cells
    row = pl.BlockSpec((1, LANES), lambda c: (0, c))
    block = pl.BlockSpec((1, phases, cells, LANES), lambda c: (0, 0, 0, c))
    return pl.pallas_call(
        functools.partial(back_kernel, half, width, len(grad_maps)),
        grid=(width // LANES,),
        in_specs=[
            block,
            pl.BlockSpec((1, blocks, 8, tokens), lambda c: (0, 0, 0, 0)),
            row,
            row,
            pl.BlockSpec((9, LANES), lambda c: (0, c)),
        ]
        + [block] * len(grad_maps),
        out_specs=[
            pl.BlockSpec((tokens, LANES), lambda c: (0, c)),
            pl.BlockSpec((16, LANES), lambda c: (0, c)),
            pl.BlockSpec((8, tokens), lambda c: (0, 0)),
        ],
        out_shape=[
            jax.ShapeDtypeStruct((tokens, width), F32),
            jax.ShapeDtypeStruct((16, width), F32),
            jax.ShapeDtypeStruct((8, tokens), F32),
        ],
        scratch_shapes=[pltpu.VMEM((tokens, LANES), F32)] * 4,
        compiler_params=params(8),
        cost_estimate=pl.CostEstimate(
            flops=150 * pre.size,
            bytes_accessed=10 * pre.size,
            transcendentals=0,
        ),
        name="back",
    )(pre, stats, gain, bias, dw, *grad_maps)


def turn_kernel(
    total_width, scaled_ref, pre_ref, stat_ref, back_ref, sums_ref, out_ref, mean_ref, rstd_ref, first_ref, second_ref
):
    tokens, width = scaled_ref.shape
    owners, rows, _ = out_ref.shape
    share = width // owners
    spread_stats(stat_ref[0], total_width, mean_ref, rstd_ref)
    column = rows_to_columns(
        jnp.sum(back_ref[...], axis=0) * (1.0 / (total_width * back_ref.shape[0]))
    )
    first_ref[...] = jnp.broadcast_to(column[0], first_ref.shape)
    second_ref[...] = jnp.broadcast_to(column[1], second_ref.shape)
    mean, rstd, first, second = mean_ref[...], rstd_ref[...], first_ref[...], second_ref[...]
    for part in range(width // LANES):
        lanes = slice(part * LANES, (part + 1) * LANES)
        normed = (pre_ref[0, :, :, lanes].reshape(tokens, LANES) - mean) * rstd
        grad = ((scaled_ref[:, lanes] - first - normed * second) * rstd).T.astype(BF)
        row = part * LANES
        while row < (part + 1) * LANES:
            owner, place = divmod(row, share)
            count = min(share - place, (part + 1) * LANES - row)
            out_ref[owner, place : place + count] = grad[row - part * LANES : row - part * LANES + count]
            row += count
    for owner in range(owners):
        if rows - 16 > share:
            out_ref[owner, share : rows - 16] = jnp.zeros((rows - 16 - share, tokens), BF)
        value = sums_ref[:, owner * share : (owner + 1) * share]
        large = value.astype(BF)
        small = (value - large.astype(F32)).astype(BF)
        edge = jnp.zeros((16, LANES - share), BF)
        out_ref[owner, rows - 16 :, :LANES] = jnp.concatenate([large, edge], axis=1)
        out_ref[owner, rows - 16 :, LANES:] = jnp.concatenate([small, edge], axis=1)


def turn_call(scaled, pre, stats, back, sums, owners):
    tokens, width = scaled.shape
    rows = -(-(width // owners) // 16) * 16 + 16
    return pl.pallas_call(
        functools.partial(turn_kernel, width),
        out_shape=jax.ShapeDtypeStruct((owners, rows, tokens), BF),
        scratch_shapes=[pltpu.VMEM((tokens, LANES), F32)] * 4,
        compiler_params=params(10),
        cost_estimate=pl.CostEstimate(
            flops=8 * scaled.size,
            bytes_accessed=10 * scaled.size,
            transcendentals=0,
        ),
        name="turn",
    )(scaled, pre, stats, back, sums)


def weight_kernel(counts, info_ref, grad_ref, *refs):
    total_pieces = sum(counts)
    pieces = refs[:total_pieces]
    out_ref, dw_ref, gain_ref, bias_ref, rows_ref, held_ref, total_ref, sems = refs[total_pieces:]
    groups, frame = len(counts), grad_ref.shape[2]
    cells = frame // 4
    share = out_ref.shape[0]
    slots = held_ref.shape[0]

    def copies(group):
        first = sum(counts[:group])
        length = frame // counts[group]
        return [
            pltpu.make_async_copy(
                pieces[first + i],
                held_ref.at[group % slots, pl.ds(i * length, length)],
                sems.at[group % slots, i],
            )
            for i in range(counts[group])
        ]

    for group in range(min(slots, groups)):
        for copy in copies(group):
            copy.start()

    own = info_ref[0]
    if share < LANES:
        rows_ref[:, share:] = jnp.zeros((groups, LANES - share, frame), BF)
    for group in range(groups):
        value = grad_ref[info_ref[1 + group], :share].astype(F32)
        if group:
            value = jnp.where((own & 2) == 2, pltpu.roll(value, 2 * cells, 1), value)
            part = lax.broadcasted_iota(jnp.int32, value.shape, 1) // cells
            swapped = jnp.where(
                (part & 1) == 0, pltpu.roll(value, 3 * cells, 1), pltpu.roll(value, cells, 1)
            )
            value = jnp.where((own & 1) == 1, swapped, value)
        rows_ref[group, :share] = value.astype(BF)
    total = jnp.zeros((16, LANES), F32)
    for group in range(groups):
        tail = grad_ref[group, grad_ref.shape[1] - 16 :].astype(F32)
        total = total + tail[:, :LANES] + tail[:, LANES : 2 * LANES]
    for row in range(3):
        dw_ref[row] = total[3 * row : 3 * row + 3, :share]
    gain_ref[...] = total[9:10, :share]
    bias_ref[...] = total[10:11, :share]

    for group in range(groups):
        for copy in copies(group):
            copy.wait()
        value = jnp.dot(rows_ref[group], held_ref[group % slots], preferred_element_type=F32)
        if group == 0:
            total_ref[...] = value
        elif group < groups - 1:
            total_ref[...] += value
        else:
            out_ref[...] = (total_ref[...] + value)[:share]
        if group + slots < groups:
            for copy in copies(group + slots):
                copy.start()


def weight_call(info, groups, grad, share):
    count, rows, tokens = grad.shape
    depth = groups[0][0].shape[1]
    pieces = [piece for group in groups for piece in group]
    slots = min(count, 8)
    return pl.pallas_call(
        functools.partial(weight_kernel, [len(group) for group in groups]),
        in_specs=[
            pl.BlockSpec(memory_space=pltpu.SMEM),
            pl.BlockSpec(memory_space=pltpu.VMEM),
        ]
        + [pl.BlockSpec(memory_space=pl.ANY)] * len(pieces),
        out_specs=[pl.BlockSpec(memory_space=pltpu.VMEM)] * 4,
        out_shape=[
            jax.ShapeDtypeStruct((share, depth), F32),
            jax.ShapeDtypeStruct((3, 3, share), F32),
            jax.ShapeDtypeStruct((1, share), F32),
            jax.ShapeDtypeStruct((1, share), F32),
        ],
        scratch_shapes=[
            pltpu.VMEM((count, LANES, tokens), BF),
            pltpu.VMEM((slots, tokens, depth), BF),
            pltpu.VMEM((LANES, depth), F32),
            pltpu.SemaphoreType.DMA((slots, 4)),
        ],
        compiler_params=params(60),
        cost_estimate=pl.CostEstimate(
            flops=2 * LANES * count * tokens * depth,
            bytes_accessed=2 * count * tokens * depth,
            transcendentals=0,
        ),
        name="weight",
    )(info, grad, *pieces)


def tie(value, *before):
    return lax.optimization_barrier((value, before))[0]


def together(*values):
    return lax.optimization_barrier(values)


def shards(patches, w_in, ln_gain, ln_bias, dw_kernel, w_tube, grad_out, clip_frames, clip_batch):
    ranks, sections, blocks = lax.axis_size("dp"), lax.axis_size("section"), lax.axis_size("mp")
    rank, side, own = lax.axis_index("dp"), lax.axis_index("section"), lax.axis_index("mp")
    grid, depth = patches.shape[2], patches.shape[4]
    half = grid // 2
    cells = half * half
    width = w_in.shape[1]
    out_width = w_tube.shape[4]
    total_pairs = grad_out.shape[0]
    share = width // (ranks * sections)
    gain, bias = ln_gain[None, :], ln_bias[None, :]
    dw = dw_kernel.reshape(9, width)
    kernel = w_tube.reshape(4, width, out_width)
    straight = jnp.arange(4, dtype=jnp.int32)
    order = own ^ straight
    swap = [(i, (i + 1) % sections) for i in range(sections)]
    source = (rank ^ jnp.arange(ranks, dtype=jnp.int32)).astype(jnp.int32)

    def over_x(value):
        return lax.ppermute(value, "mp", CROSS)

    def over_core(value):
        return lax.ppermute(value, "mp", CORE)

    def over_y(value):
        return lax.ppermute(value, "section", swap)

    def norm_stats(stat):
        return lax.all_gather(stat, "mp", axis=1)

    def over_z(value, mask):
        return lax.ppermute(value, "dp", [(i, i ^ mask) for i in range(ranks)])

    rows = patches.reshape(grid * grid, depth)
    piece = phase_call(own[None].astype(jnp.int32), rows, 1, half)
    early = over_z(piece, 1)
    other = phase_call(own[None].astype(jnp.int32) ^ 2, tie(rows, piece), 1, half)
    across, across_x = [over_y(piece)], [over_y(other)]

    weight = pair_scale(clip_frames, clip_batch, total_pairs, clip_frames.shape[0])
    upstream = (tie(grad_out, piece).astype(F32) * weight[:, None, None]).astype(BF)
    later = tie(piece, upstream)
    fetched = [over_z(later, mask) for mask in range(2, ranks)]
    even, odd = term_call(rank[None].astype(jnp.int32), upstream, kernel)
    phased = phase_call(straight[:1], tie(rows, even), 4, half)
    own_pre, own_stat = pre_call(straight, [[phased]], w_in, cells)
    own_stat = norm_stats(own_stat)
    own_stat, early, across, across_x, odd = together(own_stat, early, across, across_x, odd)
    taken = over_z(odd, 1)
    crossed = [over_x(early)]
    across.append(over_y(early))
    own_maps = maps_call(own_pre, own_stat, gain, bias, dw, half)
    own_maps, early, fetched, crossed, across = together(
        own_maps, early, fetched, crossed, across
    )

    crossed += [over_x(value) for value in fetched]
    groups = [[early, over_core(early), crossed[0], over_core(crossed[0])]]
    pre, stat = pre_call(order, groups, w_in, cells)
    pre, stat, taken = together(pre, stat, taken)
    pres, stats = [pre], [stat]
    grad_maps, rest, step = [even], even[1:], 2
    while step < ranks:
        grad_maps.append(taken)
        rest = (rest.astype(F32) + taken[1:].astype(F32)).astype(BF)
        taken = over_z(rest[::2], step)
        rest = rest[1::2]
        step *= 2
    grad_maps.append(taken)
    across += [over_y(value) for value in fetched]
    across_x.append(over_y(crossed[0]))
    pres, stats, crossed[1:], fetched, across = together(
        pres, stats, crossed[1:], fetched, across
    )
    groups += [[a, over_core(a), b, over_core(b)] for a, b in zip(fetched, crossed[1:])]
    for start in range(1, ranks - 1, 2):
        pre, stat = pre_call(order, groups[start : start + 2], w_in, cells)
        pres.append(pre)
        stats.append(stat)
    pres, stats, grad_maps = together(pres, stats, grad_maps)
    across_x += [over_y(tie(value, stats)) for value in crossed[1:-1]]
    across_x.append(over_x(tie(across[-1], stats)))

    scaled, sums, back = back_call(own_pre, own_stat, grad_maps, gain, bias, dw, half)
    stat = norm_stats(tie(jnp.concatenate(stats + [back[None]], axis=0), across_x[-1]))
    stat, back = stat[:-1], stat[-1]
    turned = turn_call(scaled, own_pre, own_stat, back, sums, ranks * sections)
    turned, stat, across, across_x = together(turned, stat, across, across_x)
    received = lax.all_to_all(turned, ("dp", "section"), 0, 0, tiled=True)
    across = [[a, over_core(a), b, over_core(b)] for a, b in zip(across, across_x)]
    maps, start = [own_maps], 0
    for pre in pres:
        part = stat[start : start + pre.shape[0]]
        maps.append(maps_call(pre, part, gain, bias, dw, half))
        start += pre.shape[0]
    grad_w_tube, partial = tube_call(source, maps, upstream, kernel, sections * blocks)
    partial, received, across = together(partial, received, across)
    partial = lax.all_to_all(partial, ("section", "mp"), 0, 0, tiled=True)
    place = jnp.concatenate([source * sections + side, source * sections + (sections - 1 - side)])
    info = jnp.concatenate([own[None], place]).astype(jnp.int32)
    grad_w_in, grad_dw, grad_gain, grad_bias = weight_call(
        info, [[phased]] + groups + across, received, share
    )
    partial, grad_w_in = together(partial, grad_w_in)
    tubes = jnp.sum(partial.astype(F32), axis=0).astype(BF).reshape(total_pairs, -1, out_width)
    return (
        tubes,
        grad_w_in.T,
        grad_gain.reshape(share),
        grad_bias.reshape(share),
        grad_dw,
        grad_w_tube.reshape(w_tube.shape),
    )


def solution(mesh):
    placed = (
        P("dp", "section", None, None, None),
        P(None, "mp"),
        P("mp"),
        P("mp"),
        P(None, None, "mp"),
        P("section", None, None, "mp", "dp"),
        P(None, None, "dp"),
        P(),
        P(),
    )
    return jax.shard_map(
        shards,
        mesh=mesh,
        in_specs=placed,
        out_specs=(
            P(None, ("section", "mp"), "dp"),
            P(None, ("mp", "dp", "section")),
            P(("mp", "dp", "section")),
            P(("mp", "dp", "section")),
            P(None, None, ("mp", "dp", "section")),
            P("section", None, None, "mp", "dp"),
        ),
        check_vma=False,
    )
```
